1024 devices in a mesh: group: 64 (over y, z), local: 16 (over x, core).
Axes of the slice: x: 8, y: 8, z: 8, core: 2. Of those that a mesh axis runs over, the one named last changes fastest.
Arguments:
- tokens: bfloat16 [8192, 3584], P(('group', 'local')), may hold values from -6 to 6
- node_picks: int32 [8192, 4], P(('group', 'local')), may hold values from 0 to 63, as said below
- gates: bfloat16 [8192, 4, 2], P(('group', 'local')), may hold values from 0.099609375 to 1
- gate_up: bfloat16 [64, 3584, 4096], P('group', None, 'local'), may hold values from -0.09375 to 0.09375
- down_weight: bfloat16 [64, 2048, 3584], P('group', None, 'local'), may hold values from -0.1875 to 0.1875
Outputs:
- mixed: bfloat16 [8192, 3584], P(('group', 'local'))
The draws below stay inside these ranges and needn't reach their ends.
Inputs may be any that keep to these rules, and one draw needn't show every extreme that they name: `node_picks`: each token names 4 different nodes. On every device, no node is named more than 1 times by that device's tokens, and some node exactly 1 times. Over the devices that share one index along local, every node is named exactly 4 * 8 times.
All inputs are finite; a program needn't handle non-finite values.
Results may differ from the reference program's by a relative error of at most 0.0058.
Values may be sent and summed in bfloat16 or wider, within the bound.
No kernel may reach another device: no remote copies, remote signals or barrier semaphores. Data moves between devices by JAX's collectives and lax.ppermute only.
A program may use at most 32 MiB of HBM per device.

```python
import math
import jax
import jax.numpy as jnp
from jax import lax

D = 3584
FF = 1024
EXPERTS_PER_NODE = 2
NODES_TOK = 4
TOK_DEV = 8
NODES = 64
TOKEN_TOTAL = 8192
N_GROUP = 64
N_LOCAL = 16


def column_order(sub_key):
    shuffled = jax.random.permutation(sub_key, N_GROUP).astype(jnp.int32)
    position = jnp.argsort(shuffled).astype(jnp.int32)
    position = position.at[1].set(-3)
    position = position.at[N_GROUP - 1].set(-2)
    position = position.at[N_GROUP // 2].set(-1)
    return jnp.argsort(position, stable=True).astype(jnp.int32)


def draw_node_picks(key, part):
    key = jax.random.fold_in(key, 7)
    column_key, order_key = jax.random.split(key)
    offsets = jax.vmap(column_order)(jax.random.split(column_key, N_LOCAL))
    slot_index = jnp.arange(NODES_TOK * TOK_DEV) % N_GROUP
    rotation_steps = offsets[:, slot_index]
    orders = jax.vmap(lambda sub_key: jax.random.permutation(sub_key, TOK_DEV))(jax.random.split(order_key, N_GROUP * N_LOCAL))
    orders = orders.reshape(N_GROUP, N_LOCAL, TOK_DEV)
    picks_index = orders[:, :, :, None] * NODES_TOK + jnp.arange(NODES_TOK)[None, None, None, :]
    shifts_full = jnp.broadcast_to(rotation_steps[None, :, None, :], (N_GROUP, N_LOCAL, TOK_DEV, NODES_TOK * TOK_DEV))
    chosen = jnp.take_along_axis(shifts_full, picks_index, axis=3)
    nodes = (jnp.arange(N_GROUP)[:, None, None, None] + chosen) % N_GROUP
    return nodes.reshape(TOKEN_TOTAL, NODES_TOK).astype(jnp.int32)


def steps_of(key, shape, pieces, smallest, high):
    gain = 1.0
    for axis_at, blocks in pieces:
        steps = jax.random.uniform(jax.random.fold_in(jax.random.fold_in(key, 6), axis_at), (blocks,), jnp.float32, smallest / len(pieces), high / len(pieces))
        gain = gain * jnp.repeat(jnp.exp(steps), shape[axis_at] // blocks).reshape((-1,) + (1,) * (len(shape) - 1 - axis_at))
    return gain


def gaussian(stream_key, shape, scale, limit, cuts=(), kind=jnp.bfloat16):
    array = jax.random.normal(stream_key, shape, jnp.float32) * scale
    if len(cuts) > 0:
        array = steps_of(stream_key, shape, cuts, -0.22, 0.18) * array
    return jnp.clip(array, min=-limit, max=limit).astype(kind)


def setup_inputs(seed: int = 0) -> dict:
    key_list = jax.random.split(jax.random.key(seed), 6)
    tokens = gaussian(key_list[0], (TOKEN_TOTAL, D), 1.0, 6.0, ((0, 1024),))
    node_picks = draw_node_picks(jax.random.fold_in(key_list[5], 71), 0)
    gates = jnp.clip(jnp.exp(math.log(1.0) - 2.306499 * jax.random.uniform(key_list[2], (TOKEN_TOTAL, NODES_TOK, EXPERTS_PER_NODE), jnp.float32) ** steps_of(key_list[2], (TOKEN_TOTAL, NODES_TOK, EXPERTS_PER_NODE), ((0, 1024),), -0.2, 0.2)), 0.099609375, 1.0).astype(jnp.bfloat16)
    gate_up = gaussian(key_list[3], (NODES, D, 2 * EXPERTS_PER_NODE * FF), D ** -0.5, 0.09375, ((0, 64), (2, 16)))
    down_weight = gaussian(key_list[4], (NODES, EXPERTS_PER_NODE * FF, D), FF ** -0.5, 0.1875, ((0, 64), (2, 16)))
    return {"tokens": tokens, "node_picks": node_picks, "gates": gates, "gate_up": gate_up, "down_weight": down_weight}


def reference(tokens, node_picks, gates, gate_up, down_weight):
    slices = N_LOCAL // EXPERTS_PER_NODE
    unit_width = FF // slices
    per_node = NODES_TOK * TOK_DEV * N_LOCAL
    flat_picks = node_picks.reshape(-1)
    flat_gates = gates.reshape(-1, EXPERTS_PER_NODE)

    def one_node(node_id):
        chosen = jnp.nonzero(flat_picks == node_id, size=per_node)[0].astype(jnp.int32)
        node_rows = tokens[chosen // NODES_TOK]
        layout = gate_up[node_id].reshape(D, EXPERTS_PER_NODE, slices, 2, unit_width)
        running = jnp.zeros((per_node, D), jnp.float32)
        for expert in range(EXPERTS_PER_NODE):
            gate_weight = layout[:, expert, :, 0, :].reshape(D, FF)
            w_up = layout[:, expert, :, 1, :].reshape(D, FF)
            gate_proj = jnp.dot(node_rows, gate_weight, preferred_element_type=jnp.float32)
            up_proj = jnp.dot(node_rows, w_up, preferred_element_type=jnp.float32)
            weight_of = flat_gates[chosen, expert].astype(jnp.float32)
            hidden = (jax.nn.silu(gate_proj) * up_proj * weight_of[:, None]).astype(jnp.bfloat16)
            down_rows = down_weight[node_id, expert * FF:(expert + 1) * FF]
            running = running + jnp.dot(hidden, down_rows, preferred_element_type=jnp.float32)
        return chosen, running.astype(jnp.bfloat16)

    chosen_all, node_parts = lax.map(one_node, jnp.arange(NODES, dtype=jnp.int32))
    visit_out = jnp.zeros((TOKEN_TOTAL * NODES_TOK, D), jnp.bfloat16)
    visit_out = visit_out.at[chosen_all.reshape(-1)].set(node_parts.reshape(-1, D))
    summed = jnp.sum(visit_out.reshape(TOKEN_TOTAL, NODES_TOK, D).astype(jnp.float32), axis=1)
    return summed.astype(jnp.bfloat16)
```

```python
import jax
import jax.numpy as jnp
from jax import lax
from jax.sharding import Mesh
from jax.sharding import PartitionSpec as P

PAD = 128
bf16, f32 = jnp.bfloat16, jnp.float32


def dot(a, b):
    return jnp.dot(a, b, preferred_element_type=f32)


def ring(block, n):
    up = [(i, (i + 1) % n) for i in range(n)]
    down = [(i, (i - 1) % n) for i in range(n)]
    rounds = [[(0, block)]]
    fwd = back = block
    for k in range(1, n // 2):
        fwd = lax.ppermute(fwd, "x", up)
        back = lax.ppermute(back, "x", down)
        rounds.append([(k, fwd), (n - k, back)])
    rounds.append([(n // 2, lax.ppermute(fwd, "x", up))])
    return rounds


def middle(rows, gu, gu_other, dn, dn_other):
    n = lax.axis_size("x")
    x, c = lax.axis_index("x"), lax.axis_index("core")
    r, width = rows.shape[0], rows.shape[1] - PAD
    expert = x // (n // 2)
    half = gu.shape[1] // 2
    hid = jnp.zeros((n, r, 2 * half), bf16)
    for blocks in ring(rows, n):
        got = jnp.concatenate([b for _, b in blocks], axis=0) if len(blocks) > 1 else blocks[0][1]
        tok = got[:, :width]
        gate = jnp.where(expert == 0, got[:, width], got[:, width + 1]).astype(f32)[:, None]
        parts = []
        for w in (gu, gu_other):
            pr = dot(tok, w)
            parts.append((jax.nn.silu(pr[:, :half]) * pr[:, half:] * gate).astype(bf16))
        a, b = parts
        h = jnp.where(c == 0, jnp.concatenate([a, b], 1), jnp.concatenate([b, a], 1))
        for j, (k, _) in enumerate(blocks):
            hid = lax.dynamic_update_slice(
                hid, h[None, j * r : (j + 1) * r], ((x - k) % n, 0, 0)
            )
    hid = hid.reshape(n * r, 2 * half)
    out = out_other = 0.0
    for blocks in ring(hid, n):
        for k, b in blocks:
            at = ((x - k) % n) * (2 * half)
            out += dot(b, lax.dynamic_slice_in_dim(dn, at, 2 * half, 0))
            out_other += dot(b, lax.dynamic_slice_in_dim(dn_other, at, 2 * half, 0))
    feats = dn.shape[1]
    both = jnp.concatenate(
        [out.reshape(n, r, feats), out_other.reshape(n, r, feats)], axis=2
    ).astype(bf16)
    back = lax.all_to_all(both, "x", split_axis=0, concat_axis=0, tiled=True)
    back = back.transpose(1, 0, 2).reshape(r, n, 2, feats)
    back = jnp.where(c == 0, back, back[:, :, ::-1])
    return back.reshape(r, width)


def shards(tokens, node_picks, gates, gate_up, down_weight):
    group = ("y", "z")
    groups = lax.axis_size(group)
    tok_count, width = tokens.shape
    visits = node_picks.shape[1]
    received = tok_count * visits
    gu, dn = gate_up[0], down_weight[0]
    swap = [(0, 1), (1, 0)]
    gu_other = lax.ppermute(gu, "core", swap)
    dn_other = lax.ppermute(dn, "core", swap)
    hot = (node_picks[None, :, :] == jnp.arange(groups, dtype=jnp.int32)[:, None, None]).astype(f32)
    place = jnp.sum(hot, axis=2).astype(bf16)
    send_gates = jnp.sum(hot[..., None] * gates.astype(f32)[None], axis=(1, 2)).astype(bf16)
    send = jnp.concatenate(
        [
            dot(place, tokens).astype(bf16),
            send_gates,
            jnp.zeros((groups, PAD - gates.shape[2]), bf16),
        ],
        axis=1,
    )
    arrived = lax.all_to_all(send[:, None], group, split_axis=0, concat_axis=0, tiled=True)[:, 0]
    live = arrived[:, width] > 0
    ids = jnp.arange(groups, dtype=jnp.int32)
    position = (
        jnp.sum(jnp.where(live[None, :] & (ids[None, :] <= ids[:, None]), 1, 0), axis=1) - 1
    )
    select = (
        (position[None, :] == jnp.arange(received, dtype=jnp.int32)[:, None]) & live[None, :]
    ).astype(bf16)
    rows = dot(select, arrived).astype(bf16)
    visit = middle(rows, gu, gu_other, dn, dn_other)
    padded = dot(select.T, visit).astype(bf16)
    returned = lax.all_to_all(padded[:, None], group, split_axis=0, concat_axis=0, tiled=True)[:, 0]
    return dot(place.T, returned).astype(bf16)


def solution(mesh):
    fine = Mesh(mesh.devices.reshape(8, 8, 8, 2), ("y", "z", "x", "core"))
    group, local = ("y", "z"), ("x", "core")
    every = group + local
    placed = (
        P(every, None),
        P(every, None),
        P(every, None, None),
        P(group, None, local),
        P(group, None, local),
    )
    return jax.shard_map(
        shards, mesh=fine, in_specs=placed, out_specs=P(every, None), check_vma=False
    )
```

```python
import jax
import jax.numpy as jnp
from jax import lax
from jax.experimental import pallas as pl
from jax.experimental.pallas import tpu as pltpu
from jax.sharding import Mesh
from jax.sharding import PartitionSpec as P

LANES = 128
bf16, f32, i32 = jnp.bfloat16, jnp.float32, jnp.int32
VMEM = pl.BlockSpec(memory_space=pltpu.VMEM)
SMEM = pl.BlockSpec(memory_space=pltpu.SMEM)
HBM = pl.BlockSpec(memory_space=pltpu.HBM)
CHUNKS = 4


def dot(a, b):
    return jnp.dot(a, b, preferred_element_type=f32)


def dot_dims(a, b, da, db):
    return lax.dot_general(a, b, (((da,), (db,)), ((), ())), preferred_element_type=f32)


def call(kernel, outs, specs, name, scratch=()):
    return pl.pallas_call(
        kernel,
        out_shape=[jax.ShapeDtypeStruct(s, d) for s, d in outs],
        in_specs=specs,
        out_specs=[VMEM] * len(outs),
        scratch_shapes=list(scratch),
        compiler_params=pltpu.CompilerParams(vmem_limit_bytes=20 * 2**20),
        name=name,
    )


def ring(block, n):
    up = [(i, (i + 1) % n) for i in range(n)]
    down = [(i, (i - 1) % n) for i in range(n)]
    got = [(0, block)]
    fwd = back = block
    for k in range(1, n // 2):
        fwd = lax.ppermute(fwd, "x", up)
        back = lax.ppermute(back, "x", down)
        got += [(k, fwd), (n - k, back)]
    got.append((n // 2, lax.ppermute(fwd, "x", up)))
    return got


def pack_kernel(picks_ref, gates_ref, tok_ref, send_ref, place_ref):
    visits, toks = picks_ref.shape
    groups, _, wide = send_ref.shape
    half = wide - LANES
    node = lax.broadcasted_iota(i32, (groups, toks), 0)
    place = jnp.zeros((groups, toks), f32)
    lane = lax.broadcasted_iota(i32, (groups, LANES), 1)
    tail = jnp.zeros((groups, LANES), f32)
    for j in range(visits):
        hot = (node == picks_ref[j : j + 1, :]).astype(f32)
        place += hot
        for e in range(gates_ref.shape[1]):
            gate = jnp.sum(hot * gates_ref[j, e : e + 1, :].astype(f32), axis=1, keepdims=True)
            tail += jnp.where(lane == e, gate, 0.0)
    place = place.astype(bf16)
    place_ref[...] = place
    for h in range(2):
        send_ref[:, h, :half] = dot(place, tok_ref[:, h * half : (h + 1) * half]).astype(bf16)
        send_ref[:, h, half:] = tail.astype(bf16)


def compact_kernel(in_ref, rows_ref, select_ref):
    groups, _, wide = in_ref.shape
    half = wide - LANES
    count = rows_ref.shape[0]
    tail = in_ref[:, 0, half:]
    live = (tail.astype(f32) > 0).astype(bf16)
    low = lax.broadcasted_iota(i32, (groups, groups), 0)
    high = lax.broadcasted_iota(i32, (groups, groups), 1)
    upto = dot((high <= low).astype(bf16), live)[:, :1]
    alive = live[:, :1].astype(f32) > 0
    position = lax.broadcasted_iota(i32, (groups, count), 1).astype(f32) + 1.0
    spread = jnp.where(alive & (upto == position), 1.0, 0.0).astype(bf16)
    select_ref[...] = spread
    for h in range(2):
        rows_ref[:, h * half : (h + 1) * half] = dot_dims(
            spread, in_ref[:, h, :half], 0, 0
        ).astype(bf16)
    rows_ref[:, 2 * half :] = dot_dims(spread, tail, 0, 0).astype(bf16)


def hidden_kernel(steps, at_ref, gu_ref, other_ref, *refs):
    blocks, (out_ref, buf, sems) = refs[:-3], refs[-3:]
    depth = gu_ref.shape[0] // CHUNKS
    copies = []
    for i, w in enumerate((gu_ref, other_ref)):
        for k in range(CHUNKS):
            part = pl.ds(k * depth, depth)
            copies.append(
                pltpu.make_async_copy(w.at[part, :], buf.at[i, part, :], sems.at[i, k])
            )
            copies[-1].start()
    n = len(blocks)
    x, c = at_ref[0], at_ref[1]
    r = blocks[0].shape[0]
    width = gu_ref.shape[0]
    units = gu_ref.shape[1] // 2
    hr = r // 2
    rows = jnp.concatenate([b[:, :width] for b in blocks], axis=0)
    tail = jnp.concatenate([b[:, width:] for b in blocks], axis=0).astype(f32)
    gate = jnp.where(x < n // 2, tail[:, 0:1], tail[:, 1:2])
    parts = []
    for i in range(2):
        pr = 0.0
        for k in range(CHUNKS):
            copies[i * CHUNKS + k].wait()
            lo, hi = k * depth, (k + 1) * depth
            pr += dot(rows[:, lo:hi], buf[i, lo:hi, :])
        g, p = pr[:, :units], pr[:, units:]
        parts.append((g / (1.0 + jnp.exp(-g)) * p * gate).astype(bf16))
    mine, other = parts
    first = jnp.where(c == 0, mine, other)
    second = jnp.where(c == 0, other, mine)
    h = jnp.concatenate([first, second], axis=1)
    for j, k in enumerate(steps):
        owner = lax.rem(x + (n - k), n)
        at = pl.ds(pl.multiple_of(owner * hr, hr), hr)
        for dest in range(n):
            lo = j * r + (dest % 2) * hr
            out_ref[dest, at, :] = h[lo : lo + hr]


def down_kernel(at_ref, h_ref, own_ref, other_ref, pair_ref, both_ref, out_ref, buf, sems):
    copies = [
        pltpu.make_async_copy(w, buf.at[i], sems.at[i])
        for i, w in enumerate((own_ref, other_ref, pair_ref, both_ref))
    ]
    for copy in copies:
        copy.start()
    n, rows, units = h_ref.shape
    b, c = lax.rem(at_ref[0], 2), at_ref[1]
    h = jnp.concatenate([h_ref[k] for k in range(n)], axis=1)
    parts = []
    for i in range(4):
        copies[i].wait()
        parts.append(dot_dims(h, buf[i], 1, 1).astype(bf16))
    hr = out_ref.shape[1]
    for bb in range(2):
        for cc in range(2):

            @pl.when((b == bb) & (c == cc))
            def _():
                order = [parts[2 * (p // 2 != bb) + (p % 2 != cc)] for p in range(4)]
                whole = jnp.concatenate(order, axis=1)
                for k in range(out_ref.shape[0]):
                    out_ref[k] = whole[k * hr : (k + 1) * hr]


def spread_kernel(back_ref, select_ref, out_ref):
    n, hr, feats = back_ref.shape
    rows = [
        jnp.concatenate([back_ref[2 * a], back_ref[2 * a + 1]], axis=0) for a in range(n // 2)
    ]
    whole = jnp.concatenate(rows, axis=1)
    half = out_ref.shape[2]
    for h in range(2):
        out_ref[:, h, :] = dot(select_ref[...], whole[:, h * half : (h + 1) * half]).astype(bf16)


def mix_kernel(in_ref, place_ref, out_ref):
    half = in_ref.shape[2]
    for h in range(2):
        out_ref[:, h * half : (h + 1) * half] = dot_dims(
            place_ref[...], in_ref[:, h, :], 0, 0
        ).astype(bf16)


def shards(tokens, node_picks, gates, gate_up, down_weight):
    group = ("y", "z")
    groups, n = lax.axis_size(group), lax.axis_size("x")
    toks, width = tokens.shape
    visits = node_picks.shape[1]
    r = toks * visits
    half = width // 2
    at = jnp.stack([lax.axis_index("x"), lax.axis_index("core")]).astype(i32)
    gu, dn = gate_up[0], down_weight[0].T
    feats, units = dn.shape[0], dn.shape[1] // n
    swap = [(0, 1), (1, 0)]
    pair = [(i, i ^ 1) for i in range(n)]
    send, place = call(
        pack_kernel,
        [((groups, 2, half + LANES), bf16), ((groups, toks), bf16)],
        [VMEM] * 3,
        "pack",
    )(node_picks.T, gates.transpose(1, 2, 0), tokens)
    dn_pair = lax.ppermute(dn, "x", pair)
    gu_other = lax.ppermute(gu, "core", swap)
    dn_other = lax.ppermute(dn, "core", swap)
    arrived = lax.all_to_all(send, group, split_axis=0, concat_axis=0, tiled=True)
    arrived, dn_pair, gu_other, dn_other = lax.optimization_barrier(
        (arrived, dn_pair, gu_other, dn_other)
    )
    dn_both = lax.ppermute(dn_pair, "core", swap)
    rows, select = call(
        compact_kernel,
        [((r, width + LANES), bf16), ((groups, r), bf16)],
        [VMEM],
        "compact",
    )(arrived)
    got = ring(rows, n)
    steps = tuple(k for k, _ in got)
    (hid,) = call(
        lambda *refs: hidden_kernel(steps, *refs),
        [((n, n * r // 2, units), bf16)],
        [SMEM, HBM, HBM] + [VMEM] * n,
        "hidden",
        [pltpu.VMEM((2,) + gu.shape, bf16), pltpu.SemaphoreType.DMA((2, CHUNKS))],
    )(at, gu, gu_other, *[b for _, b in got])
    hid = lax.all_to_all(hid, "x", split_axis=0, concat_axis=0, tiled=True)
    (out,) = call(
        down_kernel,
        [((n, r // 2, 4 * feats), bf16)],
        [SMEM, VMEM] + [HBM] * 4,
        "down",
        [pltpu.VMEM((4,) + dn.shape, bf16), pltpu.SemaphoreType.DMA((4,))],
    )(at, hid, dn, dn_other, dn_pair, dn_both)
    back = lax.all_to_all(out, "x", split_axis=0, concat_axis=0, tiled=True)
    (padded,) = call(spread_kernel, [((groups, 2, half), bf16)], [VMEM] * 2, "spread")(
        back, select
    )
    returned = lax.all_to_all(padded, group, split_axis=0, concat_axis=0, tiled=True)
    (mixed,) = call(mix_kernel, [((toks, width), bf16)], [VMEM] * 2, "mix")(returned, place)
    return mixed


def solution(mesh):
    fine = Mesh(mesh.devices.reshape(8, 8, 8, 2), ("y", "z", "x", "core"))
    group, local = ("y", "z"), ("x", "core")
    every = group + local
    placed = (
        P(every, None),
        P(every, None),
        P(every, None, None),
        P(group, None, local),
        P(group, None, local),
    )
    return jax.shard_map(
        shards, mesh=fine, in_specs=placed, out_specs=P(every, None), check_vma=False
    )
```

```python
import jax
import jax.numpy as jnp
from jax import lax
from jax.experimental import pallas as pl
from jax.experimental.pallas import tpu as pltpu
from jax.sharding import Mesh
from jax.sharding import PartitionSpec as P

LANES = 128
bf16, f32, i32 = jnp.bfloat16, jnp.float32, jnp.int32
VMEM = pl.BlockSpec(memory_space=pltpu.VMEM)
SMEM = pl.BlockSpec(memory_space=pltpu.SMEM)
HBM = pl.BlockSpec(memory_space=pltpu.HBM)
CHUNKS = 4
HID = 50
DOWN = 50


def dot(a, b):
    return jnp.dot(a, b, preferred_element_type=f32)


def dot_dims(a, b, da, db):
    return lax.dot_general(a, b, (((da,), (db,)), ((), ())), preferred_element_type=f32)


def call(kernel, outs, specs, name, scratch=(), room=8):
    return pl.pallas_call(
        kernel,
        out_shape=[jax.ShapeDtypeStruct(s, d) for s, d in outs],
        in_specs=specs,
        out_specs=[VMEM] * len(outs),
        scratch_shapes=list(scratch),
        compiler_params=pltpu.CompilerParams(vmem_limit_bytes=room * 2**20),
        name=name,
    )


def ring(block, n):
    up = [(i, (i + 1) % n) for i in range(n)]
    down = [(i, (i - 1) % n) for i in range(n)]
    got = [(0, block)]
    fwd = back = block
    for k in range(1, n // 2):
        fwd = lax.ppermute(fwd, "x", up)
        back = lax.ppermute(back, "x", down)
        got += [(k, fwd), (n - k, back)]
    got.append((n // 2, lax.ppermute(fwd, "x", up)))
    return got


def pack_kernel(picks_ref, gates_ref, tok_ref, send_ref, place_ref):
    visits, toks = picks_ref.shape
    groups, _, wide = send_ref.shape
    half = wide - LANES
    node = lax.broadcasted_iota(i32, (groups, toks), 0)
    place = jnp.zeros((groups, toks), f32)
    lane = lax.broadcasted_iota(i32, (groups, LANES), 1)
    tail = jnp.zeros((groups, LANES), f32)
    for j in range(visits):
        hot = (node == picks_ref[j : j + 1, :]).astype(f32)
        place += hot
        for e in range(gates_ref.shape[1]):
            gate = jnp.sum(hot * gates_ref[j, e : e + 1, :].astype(f32), axis=1, keepdims=True)
            tail += jnp.where(lane == e, gate, 0.0)
    place = place.astype(bf16)
    place_ref[...] = place
    for h in range(2):
        send_ref[:, h, :half] = dot(place, tok_ref[:, h * half : (h + 1) * half]).astype(bf16)
        send_ref[:, h, half:] = tail.astype(bf16)


def compact_kernel(in_ref, rows_ref, select_ref):
    groups, _, wide = in_ref.shape
    half = wide - LANES
    count = rows_ref.shape[0]
    tail = in_ref[:, 0, half:]
    live = (tail.astype(f32) > 0).astype(bf16)
    low = lax.broadcasted_iota(i32, (groups, groups), 0)
    high = lax.broadcasted_iota(i32, (groups, groups), 1)
    upto = dot((high <= low).astype(bf16), live)[:, :1]
    alive = live[:, :1].astype(f32) > 0
    position = lax.broadcasted_iota(i32, (groups, count), 1).astype(f32) + 1.0
    spread = jnp.where(alive & (upto == position), 1.0, 0.0).astype(bf16)
    select_ref[...] = spread
    for h in range(2):
        rows_ref[:, h * half : (h + 1) * half] = dot_dims(
            spread, in_ref[:, h, :half], 0, 0
        ).astype(bf16)
    rows_ref[:, 2 * half :] = dot_dims(spread, tail, 0, 0).astype(bf16)


def hidden_kernel(steps, at_ref, gu_ref, other_ref, *refs):
    blocks, (out_ref, buf, sems) = refs[:-3], refs[-3:]
    depth = gu_ref.shape[0] // CHUNKS
    copies = []
    for i, w in enumerate((gu_ref, other_ref)):
        for k in range(CHUNKS):
            part = pl.ds(k * depth, depth)
            copies.append(
                pltpu.make_async_copy(w.at[part, :], buf.at[i, part, :], sems.at[i, k])
            )
            copies[-1].start()
    n = len(blocks)
    x, c = at_ref[0], at_ref[1]
    r = blocks[0].shape[0]
    width = gu_ref.shape[0]
    units = gu_ref.shape[1] // 2
    hr = r // 2
    rows = jnp.concatenate([b[:, :width] for b in blocks], axis=0)
    tail = jnp.concatenate([b[:, width:] for b in blocks], axis=0).astype(f32)
    gate = jnp.where(x < n // 2, tail[:, 0:1], tail[:, 1:2])
    parts = []
    for i in range(2):
        pr = 0.0
        for k in range(CHUNKS):
            copies[i * CHUNKS + k].wait()
            lo, hi = k * depth, (k + 1) * depth
            pr += dot(rows[:, lo:hi], buf[i, lo:hi, :])
        g, p = pr[:, :units], pr[:, units:]
        parts.append((g / (1.0 + jnp.exp(-g)) * p * gate).astype(bf16))
    mine, other = parts
    first = jnp.where(c == 0, mine, other)
    second = jnp.where(c == 0, other, mine)
    h = jnp.concatenate([first, second], axis=1)
    for j, k in enumerate(steps):
        owner = lax.rem(x + (n - k), n)
        at = pl.ds(pl.multiple_of(owner * hr, hr), hr)
        for dest in range(n):
            lo = j * r + (dest % 2) * hr
            out_ref[dest, at, :] = h[lo : lo + hr]


def down_kernel(at_ref, h_ref, own_ref, other_ref, pair_ref, both_ref, out_ref, buf, sems):
    copies = [
        pltpu.make_async_copy(w, buf.at[i], sems.at[i])
        for i, w in enumerate((own_ref, other_ref, pair_ref, both_ref))
    ]
    for copy in copies:
        copy.start()
    n, rows, units = h_ref.shape
    b, c = lax.rem(at_ref[0], 2), at_ref[1]
    h = jnp.concatenate([h_ref[k] for k in range(n)], axis=1)
    parts = []
    for i in range(4):
        copies[i].wait()
        parts.append(dot_dims(h, buf[i], 1, 1).astype(bf16))
    hr = out_ref.shape[1]
    for bb in range(2):
        for cc in range(2):

            @pl.when((b == bb) & (c == cc))
            def _():
                order = [parts[2 * (p // 2 != bb) + (p % 2 != cc)] for p in range(4)]
                whole = jnp.concatenate(order, axis=1)
                for k in range(out_ref.shape[0]):
                    out_ref[k] = whole[k * hr : (k + 1) * hr]


def spread_kernel(back_ref, select_ref, out_ref):
    n, hr, feats = back_ref.shape
    rows = [
        jnp.concatenate([back_ref[2 * a], back_ref[2 * a + 1]], axis=0) for a in range(n // 2)
    ]
    whole = jnp.concatenate(rows, axis=1)
    half = out_ref.shape[2]
    for h in range(2):
        out_ref[:, h, :] = dot(select_ref[...], whole[:, h * half : (h + 1) * half]).astype(bf16)


def mix_kernel(in_ref, place_ref, out_ref):
    half = in_ref.shape[2]
    for h in range(2):
        out_ref[:, h * half : (h + 1) * half] = dot_dims(
            place_ref[...], in_ref[:, h, :], 0, 0
        ).astype(bf16)


def shards(tokens, node_picks, gates, gate_up, down_weight):
    group = ("y", "z")
    groups, n = lax.axis_size(group), lax.axis_size("x")
    toks, width = tokens.shape
    visits = node_picks.shape[1]
    r = toks * visits
    half = width // 2
    at = jnp.stack([lax.axis_index("x"), lax.axis_index("core")]).astype(i32)
    gu, dn = gate_up[0], down_weight[0].T
    feats, units = dn.shape[0], dn.shape[1] // n
    swap = [(0, 1), (1, 0)]
    pair = [(i, i ^ 1) for i in range(n)]
    send, place = call(
        pack_kernel,
        [((groups, 2, half + LANES), bf16), ((groups, toks), bf16)],
        [VMEM] * 3,
        "pack",
        room=60,
    )(node_picks.T, gates.transpose(1, 2, 0), tokens)
    dn_pair = lax.ppermute(dn, "x", pair)
    gu_other = lax.ppermute(gu, "core", swap)
    dn_other = lax.ppermute(dn, "core", swap)
    arrived = lax.all_to_all(send, group, split_axis=0, concat_axis=0, tiled=True)
    dn_both = lax.ppermute(dn_pair, "core", swap)
    arrived, dn_pair, gu_other, dn_other, dn_both = lax.optimization_barrier(
        (arrived, dn_pair, gu_other, dn_other, dn_both)
    )
    rows, select = call(
        compact_kernel,
        [((r, width + LANES), bf16), ((groups, r), bf16)],
        [VMEM],
        "compact",
    )(arrived)
    got = ring(rows, n)
    steps = tuple(k for k, _ in got)
    (hid,) = call(
        lambda *refs: hidden_kernel(steps, *refs),
        [((n, n * r // 2, units), bf16)],
        [SMEM, HBM, HBM] + [VMEM] * n,
        "hidden",
        [pltpu.VMEM((2,) + gu.shape, bf16), pltpu.SemaphoreType.DMA((2, CHUNKS))],
        HID,
    )(at, gu, gu_other, *[b for _, b in got])
    hid = lax.all_to_all(hid, "x", split_axis=0, concat_axis=0, tiled=True)
    (out,) = call(
        down_kernel,
        [((n, r // 2, 4 * feats), bf16)],
        [SMEM, VMEM] + [HBM] * 4,
        "down",
        [pltpu.VMEM((4,) + dn.shape, bf16), pltpu.SemaphoreType.DMA((4,))],
        DOWN,
    )(at, hid, dn, dn_other, dn_pair, dn_both)
    back = lax.all_to_all(out, "x", split_axis=0, concat_axis=0, tiled=True)
    (padded,) = call(spread_kernel, [((groups, 2, half), bf16)], [VMEM] * 2, "spread")(
        back, select
    )
    returned = lax.all_to_all(padded, group, split_axis=0, concat_axis=0, tiled=True)
    (mixed,) = call(mix_kernel, [((toks, width), bf16)], [VMEM] * 2, "mix")(returned, place)
    return mixed


def solution(mesh):
    fine = Mesh(mesh.devices.reshape(8, 8, 8, 2), ("y", "z", "x", "core"))
    group, local = ("y", "z"), ("x", "core")
    every = group + local
    placed = (
        P(every, None),
        P(every, None),
        P(every, None, None),
        P(group, None, local),
        P(group, None, local),
    )
    return jax.shard_map(
        shards, mesh=fine, in_specs=placed, out_specs=P(every, None), check_vma=False
    )
```

```python
import functools

import jax
import jax.numpy as jnp
from jax import lax
from jax.experimental import pallas as pl
from jax.experimental.pallas import tpu as pltpu
from jax.sharding import Mesh
from jax.sharding import PartitionSpec as P

LANES = 128
bf16, f32, i32 = jnp.bfloat16, jnp.float32, jnp.int32
VMEM = pl.BlockSpec(memory_space=pltpu.VMEM)
SMEM = pl.BlockSpec(memory_space=pltpu.SMEM)
HBM = pl.BlockSpec(memory_space=pltpu.HBM)
CHUNKS = 4
HID = 50
LAST = 60
DOWN = 50


def dot(a, b):
    return jnp.dot(a, b, preferred_element_type=f32)


def dot_dims(a, b, da, db):
    return lax.dot_general(a, b, (((da,), (db,)), ((), ())), preferred_element_type=f32)


def call(kernel, outs, specs, name, scratch=(), room=8):
    return pl.pallas_call(
        kernel,
        out_shape=[jax.ShapeDtypeStruct(s, d) for s, d in outs],
        in_specs=specs,
        out_specs=[VMEM] * len(outs),
        scratch_shapes=list(scratch),
        compiler_params=pltpu.CompilerParams(vmem_limit_bytes=room * 2**20),
        name=name,
    )


def ring(block, n):
    up = [(i, (i + 1) % n) for i in range(n)]
    down = [(i, (i - 1) % n) for i in range(n)]
    got = [(0, block)]
    fwd = back = block
    for k in range(1, n // 2):
        fwd = lax.ppermute(fwd, "x", up)
        back = lax.ppermute(back, "x", down)
        got += [(k, fwd), (n - k, back)]
    got.append((n // 2, lax.ppermute(fwd, "x", up)))
    return got


def pack_kernel(picks_ref, gates_ref, tok_ref, send_ref, place_ref):
    visits, toks = picks_ref.shape
    groups, _, wide = send_ref.shape
    half = wide - LANES
    node = lax.broadcasted_iota(i32, (groups, toks), 0)
    place = jnp.zeros((groups, toks), f32)
    lane = lax.broadcasted_iota(i32, (groups, LANES), 1)
    tail = jnp.zeros((groups, LANES), f32)
    for j in range(visits):
        hot = (node == picks_ref[j : j + 1, :]).astype(f32)
        place += hot
        for e in range(gates_ref.shape[1]):
            gate = jnp.sum(hot * gates_ref[j, e : e + 1, :].astype(f32), axis=1, keepdims=True)
            tail += jnp.where(lane == e, gate, 0.0)
    place = place.astype(bf16)
    place_ref[...] = place
    for h in range(2):
        send_ref[:, h, :half] = dot(place, tok_ref[:, h * half : (h + 1) * half]).astype(bf16)
        send_ref[:, h, half:] = tail.astype(bf16)


def by_half(hot):
    slots, k = hot.shape
    twice = jnp.broadcast_to(hot[:, None, :], (slots, 2, k)).reshape(2 * slots, k)
    parity = lax.broadcasted_iota(i32, (2 * slots, k), 0) % 2
    return jnp.concatenate([jnp.where(parity == h, twice, 0.0) for h in range(2)], axis=1).astype(
        bf16
    )


def compact_kernel(in_ref, rows_ref, select_ref):
    groups, _, wide = in_ref.shape
    half = wide - LANES
    count = rows_ref.shape[0]
    tail = in_ref[:, 0, half:]
    live = (tail.astype(f32) > 0).astype(bf16)
    low = lax.broadcasted_iota(i32, (groups, groups), 0)
    high = lax.broadcasted_iota(i32, (groups, groups), 1)
    upto = dot((high <= low).astype(bf16), live)[:, :1]
    alive = live[:, :1].astype(f32) > 0
    position = lax.broadcasted_iota(i32, (groups, count), 1).astype(f32) + 1.0
    spread = jnp.where(alive & (upto == position), 1.0, 0.0)
    select_ref[...] = spread.astype(bf16)
    both = dot_dims(by_half(spread), in_ref[...].reshape(2 * groups, wide), 0, 0).astype(bf16)
    rows_ref[:, :half] = both[:count, :half]
    rows_ref[:, half : 2 * half] = both[count:, :half]
    rows_ref[:, 2 * half :] = both[:count, half:]


def hidden_kernel(steps, at_ref, gu_ref, other_ref, *refs):
    out_ref, buf, sems = refs[-3:]
    depth = gu_ref.shape[0] // CHUNKS
    copies = []
    for k in range(CHUNKS):
        for i, w in enumerate((gu_ref, other_ref)):
            part = pl.ds(k * depth, depth)
            copies.append(
                pltpu.make_async_copy(w.at[part, :], buf.at[i, part, :], sems.at[i, k])
            )
            copies[-1].start()
    done = refs[0] if steps else None
    blocks = refs[1:-3] if steps else refs[:-3]
    x, c = at_ref[0], at_ref[1]
    r = blocks[0].shape[0]
    width = gu_ref.shape[0]
    units = gu_ref.shape[1] // 2
    rows = jnp.concatenate([b[:, :width] for b in blocks], axis=0)
    tail = jnp.concatenate([b[:, width:] for b in blocks], axis=0).astype(f32)
    gate = jnp.where(at_ref[2] == 0, tail[:, 0:1], tail[:, 1:2])
    prs = [0.0, 0.0]
    for k in range(CHUNKS):
        for i in range(2):
            copies[2 * k + i].wait()
            lo, hi = k * depth, (k + 1) * depth
            prs[i] += dot(rows[:, lo:hi], buf[i, lo:hi, :])
    parts = []
    for pr in prs:
        g, p = pr[:, :units], pr[:, units:]
        parts.append((g / (1.0 + jnp.exp(-g)) * p * gate).astype(bf16))
    mine, other = parts
    first = jnp.where(c == 0, mine, other)
    second = jnp.where(c == 0, other, mine)
    h = jnp.concatenate([first, second], axis=1)
    if not steps:
        out_ref[...] = h
        return
    n, hr = len(steps), r // 2
    for j, k in enumerate(steps):
        owner = lax.rem(x + (n - k), n)
        at = pl.ds(pl.multiple_of(owner * hr, hr), hr)
        for b in range(2):
            if j < n - 1:
                part = done[j * r + b * hr : j * r + (b + 1) * hr, :]
            else:
                part = h[b * hr : (b + 1) * hr]
            for dest in range(b, n, 2):
                out_ref[dest, at, :] = part


def down_kernel(at_ref, h_ref, own_ref, other_ref, pair_ref, both_ref, out_ref):
    n, rows, units = h_ref.shape
    b, c = lax.rem(at_ref[0], 2), at_ref[1]
    h = jnp.concatenate([h_ref[k] for k in range(n)], axis=1)
    parts = [
        dot_dims(h, w[...], 1, 1).astype(bf16) for w in (own_ref, other_ref, pair_ref, both_ref)
    ]
    hr = out_ref.shape[1]
    for bb in range(2):
        for cc in range(2):

            @pl.when((b == bb) & (c == cc))
            def _():
                order = [parts[2 * (p // 2 != bb) + (p % 2 != cc)] for p in range(4)]
                whole = jnp.concatenate(order, axis=1)
                for k in range(out_ref.shape[0]):
                    out_ref[k] = whole[k * hr : (k + 1) * hr]


def spread_kernel(back_ref, select_ref, out_ref):
    n, hr, feats = back_ref.shape
    rows = [
        jnp.concatenate([back_ref[2 * a], back_ref[2 * a + 1]], axis=0) for a in range(n // 2)
    ]
    whole = jnp.concatenate(rows, axis=1)
    half = out_ref.shape[2]
    for h in range(2):
        out_ref[:, h, :] = dot(select_ref[...], whole[:, h * half : (h + 1) * half]).astype(bf16)


def mix_kernel(in_ref, place_ref, out_ref):
    slots, _, half = in_ref.shape
    toks = out_ref.shape[0]
    lhs = by_half(place_ref[...].astype(f32))
    both = dot_dims(lhs, in_ref[...].reshape(2 * slots, half), 0, 0).astype(bf16)
    out_ref[:, :half] = both[:toks]
    out_ref[:, half:] = both[toks:]


def shards(tokens, node_picks, gates, gate_up, down_weight):
    group = ("y", "z")
    groups, n = lax.axis_size(group), lax.axis_size("x")
    toks, width = tokens.shape
    visits = node_picks.shape[1]
    r = toks * visits
    half = width // 2
    x = lax.axis_index("x")
    at = jnp.stack([x, lax.axis_index("core"), x // (n // 2)]).astype(i32)
    gu, dn = gate_up[0], down_weight[0].T
    feats, units = dn.shape[0], dn.shape[1] // n
    swap = [(0, 1), (1, 0)]
    pair = [(i, i ^ 1) for i in range(n)]
    send, place = call(
        pack_kernel,
        [((groups, 2, half + LANES), bf16), ((groups, toks), bf16)],
        [VMEM] * 3,
        "pack",
        room=60,
    )(node_picks.T, gates.transpose(1, 2, 0), tokens)
    dn_pair = lax.ppermute(dn, "x", pair)
    gu_other = lax.ppermute(gu, "core", swap)
    dn_other = lax.ppermute(dn, "core", swap)
    arrived = lax.all_to_all(send, group, split_axis=0, concat_axis=0, tiled=True)
    dn_both = lax.ppermute(dn_pair, "core", swap)
    arrived, dn_pair, dn_other, dn_both = lax.optimization_barrier(
        (arrived, dn_pair, dn_other, dn_both)
    )
    rows, select = call(
        compact_kernel,
        [((r, width + LANES), bf16), ((groups, r), bf16)],
        [VMEM],
        "compact",
    )(arrived)
    got = ring(rows, n)
    steps = tuple(k for k, _ in got)
    *early, last = [b for _, b in got]
    scratch = [pltpu.VMEM((2,) + gu.shape, bf16), pltpu.SemaphoreType.DMA((2, CHUNKS))]
    (done,) = call(
        functools.partial(hidden_kernel, ()),
        [((len(early) * r, units), bf16)],
        [SMEM, HBM, HBM] + [VMEM] * len(early),
        "hidden_early",
        scratch,
        HID,
    )(at, gu, gu_other, *early)
    (hid,) = call(
        functools.partial(hidden_kernel, steps),
        [((n, n * r // 2, units), bf16)],
        [SMEM, HBM, HBM] + [VMEM] * 2,
        "hidden_last",
        scratch,
        LAST,
    )(at, gu, gu_other, done, last)
    hid = lax.all_to_all(hid, "x", split_axis=0, concat_axis=0, tiled=True)
    (out,) = call(
        down_kernel,
        [((n, r // 2, 4 * feats), bf16)],
        [SMEM] + [VMEM] * 5,
        "down",
        room=DOWN,
    )(at, hid, dn, dn_other, dn_pair, dn_both)
    back = lax.all_to_all(out, "x", split_axis=0, concat_axis=0, tiled=True)
    (padded,) = call(spread_kernel, [((groups, 2, half), bf16)], [VMEM] * 2, "spread")(
        back, select
    )
    returned = lax.all_to_all(padded, group, split_axis=0, concat_axis=0, tiled=True)
    (mixed,) = call(mix_kernel, [((toks, width), bf16)], [VMEM] * 2, "mix")(returned, place)
    return mixed


def solution(mesh):
    fine = Mesh(mesh.devices.reshape(8, 8, 8, 2), ("y", "z", "x", "core"))
    group, local = ("y", "z"), ("x", "core")
    every = group + local
    placed = (
        P(every, None),
        P(every, None),
        P(every, None, None),
        P(group, None, local),
        P(group, None, local),
    )
    return jax.shard_map(
        shards, mesh=fine, in_specs=placed, out_specs=P(every, None), check_vma=False
    )
```

```python
import functools

import jax
import jax.numpy as jnp
from jax import lax
from jax.experimental import pallas as pl
from jax.experimental.pallas import tpu as pltpu
from jax.sharding import Mesh
from jax.sharding import PartitionSpec as P

LANES = 128
bf16, f32, i32 = jnp.bfloat16, jnp.float32, jnp.int32
VMEM = pl.BlockSpec(memory_space=pltpu.VMEM)
SMEM = pl.BlockSpec(memory_space=pltpu.SMEM)
HBM = pl.BlockSpec(memory_space=pltpu.HBM)
HID = 50
DOWN = 50
BESIDE = 2


def dot(a, b):
    return jnp.dot(a, b, preferred_element_type=f32)


def dot_dims(a, b, da, db):
    return lax.dot_general(a, b, (((da,), (db,)), ((), ())), preferred_element_type=f32)


def call(kernel, outs, specs, name, scratch=(), room=8):
    return pl.pallas_call(
        kernel,
        out_shape=[jax.ShapeDtypeStruct(s, d) for s, d in outs],
        in_specs=specs,
        out_specs=[VMEM] * len(outs),
        scratch_shapes=list(scratch),
        compiler_params=pltpu.CompilerParams(vmem_limit_bytes=room * 2**20),
        name=name,
    )


def ring(block, n, beside):
    up = [(i, (i + 1) % n) for i in range(n)]
    down = [(i, (i - 1) % n) for i in range(n)]
    got = [(0, block)]
    fwd = back = block
    for k in range(1, n // 2):
        fwd = lax.ppermute(fwd, "x", up)
        back = lax.ppermute(back, "x", down)
        if k == BESIDE:
            fwd, back, beside = lax.optimization_barrier((fwd, back, beside))
        got += [(k, fwd), (n - k, back)]
    got.append((n // 2, lax.ppermute(fwd, "x", up)))
    return got, beside


def pack_kernel(picks_ref, gates_ref, tok_ref, send_ref, place_ref):
    visits, toks = picks_ref.shape
    groups, _, wide = send_ref.shape
    half = wide - LANES
    node = lax.broadcasted_iota(i32, (groups, toks), 0)
    place = jnp.zeros((groups, toks), f32)
    lane = lax.broadcasted_iota(i32, (groups, LANES), 1)
    tail = jnp.zeros((groups, LANES), f32)
    for j in range(visits):
        hot = (node == picks_ref[j : j + 1, :]).astype(f32)
        place += hot
        for e in range(gates_ref.shape[1]):
            gate = jnp.sum(hot * gates_ref[j, e : e + 1, :].astype(f32), axis=1, keepdims=True)
            tail += jnp.where(lane == e, gate, 0.0)
    place = place.astype(bf16)
    place_ref[...] = place
    for h in range(2):
        send_ref[:, h, :half] = dot(place, tok_ref[:, h * half : (h + 1) * half]).astype(bf16)
        send_ref[:, h, half:] = tail.astype(bf16)


def by_half(hot):
    slots, k = hot.shape
    twice = jnp.broadcast_to(hot[:, None, :], (slots, 2, k)).reshape(2 * slots, k)
    parity = lax.broadcasted_iota(i32, (2 * slots, k), 0) % 2
    return jnp.concatenate([jnp.where(parity == h, twice, 0.0) for h in range(2)], axis=1).astype(
        bf16
    )


def compact_kernel(in_ref, rows_ref, select_ref):
    groups, _, wide = in_ref.shape
    half = wide - LANES
    count = rows_ref.shape[0]
    tail = in_ref[:, 0, half:]
    live = (tail.astype(f32) > 0).astype(bf16)
    low = lax.broadcasted_iota(i32, (groups, groups), 0)
    high = lax.broadcasted_iota(i32, (groups, groups), 1)
    upto = dot((high <= low).astype(bf16), live)[:, :1]
    alive = live[:, :1].astype(f32) > 0
    position = lax.broadcasted_iota(i32, (groups, count), 1).astype(f32) + 1.0
    spread = jnp.where(alive & (upto == position), 1.0, 0.0)
    select_ref[...] = spread.astype(bf16)
    both = dot_dims(by_half(spread), in_ref[...].reshape(2 * groups, wide), 0, 0).astype(bf16)
    rows_ref[:, :half] = both[:count, :half]
    rows_ref[:, half : 2 * half] = both[count:, :half]
    rows_ref[:, 2 * half :] = both[:count, half:]


def hidden_kernel(steps, at_ref, gu_ref, other_ref, *refs):
    blocks, (out_ref, buf, sems) = refs[:-3], refs[-3:]
    copies = []
    for i, w in enumerate((gu_ref, other_ref)):
        copies.append(pltpu.make_async_copy(w, buf.at[i], sems.at[i]))
        copies[-1].start()
    n = len(blocks)
    x, c = at_ref[0], at_ref[1]
    r = blocks[0].shape[0]
    width = gu_ref.shape[0]
    units = gu_ref.shape[1] // 2
    hr = r // 2
    rows = jnp.concatenate([b[:, :width] for b in blocks], axis=0)
    tail = jnp.concatenate([b[:, width:] for b in blocks], axis=0).astype(f32)
    gate = jnp.where(at_ref[2] == 0, tail[:, 0:1], tail[:, 1:2])
    parts = []
    for i in range(2):
        copies[i].wait()
        pr = dot(rows, buf[i])
        g, p = pr[:, :units], pr[:, units:]
        parts.append((g / (1.0 + jnp.exp(-g)) * p * gate).astype(bf16))
    mine, other = parts
    first = jnp.where(c == 0, mine, other)
    second = jnp.where(c == 0, other, mine)
    h = jnp.concatenate([first, second], axis=1)
    for j, k in enumerate(steps):
        owner = lax.rem(x + (n - k), n)
        at = pl.ds(pl.multiple_of(owner * hr, hr), hr)
        for dest in range(n):
            lo = j * r + (dest % 2) * hr
            out_ref[dest, at, :] = h[lo : lo + hr]


def down_kernel(at_ref, h_ref, own_ref, other_ref, pair_ref, both_ref, out_ref):
    n, rows, units = h_ref.shape
    b, c = lax.rem(at_ref[0], 2), at_ref[1]
    h = jnp.concatenate([h_ref[k] for k in range(n)], axis=1)
    parts = [
        dot_dims(h, w[...], 1, 1).astype(bf16) for w in (own_ref, other_ref, pair_ref, both_ref)
    ]
    hr = out_ref.shape[1]
    for bb in range(2):
        for cc in range(2):

            @pl.when((b == bb) & (c == cc))
            def _():
                order = [parts[2 * (p // 2 != bb) + (p % 2 != cc)] for p in range(4)]
                whole = jnp.concatenate(order, axis=1)
                for k in range(out_ref.shape[0]):
                    out_ref[k] = whole[k * hr : (k + 1) * hr]


def spread_kernel(back_ref, select_ref, out_ref):
    n, hr, feats = back_ref.shape
    rows = [
        jnp.concatenate([back_ref[2 * a], back_ref[2 * a + 1]], axis=0) for a in range(n // 2)
    ]
    whole = jnp.concatenate(rows, axis=1)
    half = out_ref.shape[2]
    for h in range(2):
        out_ref[:, h, :] = dot(select_ref[...], whole[:, h * half : (h + 1) * half]).astype(bf16)


def mix_kernel(in_ref, place_ref, out_ref):
    slots, _, half = in_ref.shape
    toks = out_ref.shape[0]
    lhs = by_half(place_ref[...].astype(f32))
    both = dot_dims(lhs, in_ref[...].reshape(2 * slots, half), 0, 0).astype(bf16)
    out_ref[:, :half] = both[:toks]
    out_ref[:, half:] = both[toks:]


def shards(tokens, node_picks, gates, gate_up, down_weight):
    group = ("y", "z")
    groups, n = lax.axis_size(group), lax.axis_size("x")
    toks, width = tokens.shape
    visits = node_picks.shape[1]
    r = toks * visits
    half = width // 2
    x = lax.axis_index("x")
    at = jnp.stack([x, lax.axis_index("core"), x // (n // 2)]).astype(i32)
    gu, dn = gate_up[0], down_weight[0].T
    feats, units = dn.shape[0], dn.shape[1] // n
    swap = [(0, 1), (1, 0)]
    pair = [(i, i ^ 1) for i in range(n)]
    send, place = call(
        pack_kernel,
        [((groups, 2, half + LANES), bf16), ((groups, toks), bf16)],
        [VMEM] * 3,
        "pack",
        room=60,
    )(node_picks.T, gates.transpose(1, 2, 0), tokens)
    dn_pair = lax.ppermute(dn, "x", pair)
    gu_other = lax.ppermute(gu, "core", swap)
    arrived = lax.all_to_all(send, group, split_axis=0, concat_axis=0, tiled=True)
    rows, select = call(
        compact_kernel,
        [((r, width + LANES), bf16), ((groups, r), bf16)],
        [VMEM],
        "compact",
    )(arrived)
    got, dn_pair = ring(rows, n, dn_pair)
    steps = tuple(k for k, _ in got)
    (hid,) = call(
        functools.partial(hidden_kernel, steps),
        [((n, n * r // 2, units), bf16)],
        [SMEM, HBM, HBM] + [VMEM] * n,
        "hidden",
        [pltpu.VMEM((2,) + gu.shape, bf16), pltpu.SemaphoreType.DMA((2,))],
        HID,
    )(at, gu, gu_other, *[b for _, b in got])
    hid, mine, dn_pair = lax.optimization_barrier((hid, dn, dn_pair))
    dn_other = lax.ppermute(mine, "core", swap)
    dn_both = lax.ppermute(dn_pair, "core", swap)
    hid = lax.all_to_all(hid, "x", split_axis=0, concat_axis=0, tiled=True)
    (out,) = call(
        down_kernel,
        [((n, r // 2, 4 * feats), bf16)],
        [SMEM] + [VMEM] * 5,
        "down",
        room=DOWN,
    )(at, hid, dn, dn_other, dn_pair, dn_both)
    back = lax.all_to_all(out, "x", split_axis=0, concat_axis=0, tiled=True)
    (padded,) = call(spread_kernel, [((groups, 2, half), bf16)], [VMEM] * 2, "spread")(
        back, select
    )
    returned = lax.all_to_all(padded, group, split_axis=0, concat_axis=0, tiled=True)
    (mixed,) = call(mix_kernel, [((toks, width), bf16)], [VMEM] * 2, "mix")(returned, place)
    return mixed


def solution(mesh):
    fine = Mesh(mesh.devices.reshape(8, 8, 8, 2), ("y", "z", "x", "core"))
    group, local = ("y", "z"), ("x", "core")
    every = group + local
    placed = (
        P(every, None),
        P(every, None),
        P(every, None, None),
        P(group, None, local),
        P(group, None, local),
    )
    return jax.shard_map(
        shards, mesh=fine, in_specs=placed, out_specs=P(every, None), check_vma=False
    )
```

```python
import functools

import jax
import jax.numpy as jnp
from jax import lax
from jax.experimental import pallas as pl
from jax.experimental.pallas import tpu as pltpu
from jax.sharding import Mesh
from jax.sharding import PartitionSpec as P

LANES = 128
bf16, f32, i32 = jnp.bfloat16, jnp.float32, jnp.int32
VMEM = pl.BlockSpec(memory_space=pltpu.VMEM)
SMEM = pl.BlockSpec(memory_space=pltpu.SMEM)
HBM = pl.BlockSpec(memory_space=pltpu.HBM)
HID = 50
DOWN = 52
CHUNKS = 4


def dot(a, b):
    return jnp.dot(a, b, preferred_element_type=f32)


def dot_dims(a, b, da, db):
    return lax.dot_general(a, b, (((da,), (db,)), ((), ())), preferred_element_type=f32)


def call(kernel, outs, specs, name, scratch=(), room=8):
    return pl.pallas_call(
        kernel,
        out_shape=[jax.ShapeDtypeStruct(s, d) for s, d in outs],
        in_specs=specs,
        out_specs=[VMEM] * len(outs),
        scratch_shapes=list(scratch),
        compiler_params=pltpu.CompilerParams(vmem_limit_bytes=room * 2**20),
        name=name,
    )


def ring(block, n):
    up = [(i, (i + 1) % n) for i in range(n)]
    down = [(i, (i - 1) % n) for i in range(n)]
    got = [(0, block)]
    fwd = back = block
    for k in range(1, n // 2):
        fwd = lax.ppermute(fwd, "x", up)
        back = lax.ppermute(back, "x", down)
        got += [(k, fwd), (n - k, back)]
    got.append((n // 2, lax.ppermute(fwd, "x", up)))
    return got


def pack_kernel(picks_ref, gates_ref, tok_ref, send_ref, place_ref):
    visits, toks = picks_ref.shape
    groups, _, wide = send_ref.shape
    half = wide - LANES
    node = lax.broadcasted_iota(i32, (groups, toks), 0)
    place = jnp.zeros((groups, toks), f32)
    lane = lax.broadcasted_iota(i32, (groups, LANES), 1)
    tail = jnp.zeros((groups, LANES), f32)
    for j in range(visits):
        hot = (node == picks_ref[j : j + 1, :]).astype(f32)
        place += hot
        for e in range(gates_ref.shape[1]):
            gate = jnp.sum(hot * gates_ref[j, e : e + 1, :].astype(f32), axis=1, keepdims=True)
            tail += jnp.where(lane == e, gate, 0.0)
    place = place.astype(bf16)
    place_ref[...] = place
    for h in range(2):
        send_ref[:, h, :half] = dot(place, tok_ref[:, h * half : (h + 1) * half]).astype(bf16)
        send_ref[:, h, half:] = tail.astype(bf16)


def by_half(hot):
    slots, k = hot.shape
    twice = jnp.broadcast_to(hot[:, None, :], (slots, 2, k)).reshape(2 * slots, k)
    parity = lax.broadcasted_iota(i32, (2 * slots, k), 0) % 2
    return jnp.concatenate([jnp.where(parity == h, twice, 0.0) for h in range(2)], axis=1).astype(
        bf16
    )


def compact_kernel(in_ref, rows_ref, select_ref):
    groups, _, wide = in_ref.shape
    half = wide - LANES
    count = rows_ref.shape[0]
    tail = in_ref[:, 0, half:]
    live = (tail.astype(f32) > 0).astype(bf16)
    low = lax.broadcasted_iota(i32, (groups, groups), 0)
    high = lax.broadcasted_iota(i32, (groups, groups), 1)
    upto = dot((high <= low).astype(bf16), live)[:, :1]
    alive = live[:, :1].astype(f32) > 0
    position = lax.broadcasted_iota(i32, (groups, count), 1).astype(f32) + 1.0
    spread = jnp.where(alive & (upto == position), 1.0, 0.0)
    select_ref[...] = spread.astype(bf16)
    both = dot_dims(by_half(spread), in_ref[...].reshape(2 * groups, wide), 0, 0).astype(bf16)
    rows_ref[:, :half] = both[:count, :half]
    rows_ref[:, half : 2 * half] = both[count:, :half]
    rows_ref[:, 2 * half :] = both[:count, half:]


def hidden_kernel(steps, at_ref, gu_ref, other_ref, *refs):
    blocks, (out_ref, buf, sems) = refs[:-3], refs[-3:]
    depth = gu_ref.shape[0] // CHUNKS
    copies = []
    for i, w in enumerate((gu_ref, other_ref)):
        for k in range(CHUNKS):
            part = pl.ds(k * depth, depth)
            copies.append(
                pltpu.make_async_copy(w.at[part, :], buf.at[i, part, :], sems.at[i, k])
            )
            copies[-1].start()
    n = len(blocks)
    x, c = at_ref[0], at_ref[1]
    r = blocks[0].shape[0]
    width = gu_ref.shape[0]
    units = gu_ref.shape[1] // 2
    hr = r // 2
    rows = jnp.concatenate([b[:, :width] for b in blocks], axis=0)
    tail = jnp.concatenate([b[:, width:] for b in blocks], axis=0).astype(f32)
    gate = jnp.where(at_ref[2] == 0, tail[:, 0:1], tail[:, 1:2])
    parts = []
    for i in range(2):
        pr = 0.0
        for k in range(CHUNKS):
            copies[i * CHUNKS + k].wait()
            lo, hi = k * depth, (k + 1) * depth
            pr += dot(rows[:, lo:hi], buf[i, lo:hi, :])
        g, p = pr[:, :units], pr[:, units:]
        parts.append((g / (1.0 + jnp.exp(-g)) * p * gate).astype(bf16))
    mine, other = parts
    first = jnp.where(c == 0, mine, other)
    second = jnp.where(c == 0, other, mine)
    h = jnp.concatenate([first, second], axis=1)
    for j, k in enumerate(steps):
        owner = lax.rem(x + (n - k), n)
        at = pl.ds(pl.multiple_of(owner * hr, hr), hr)
        for dest in range(n):
            lo = j * r + (dest % 2) * hr
            out_ref[dest, at, :] = h[lo : lo + hr]


def down_kernel(at_ref, h_ref, own_ref, other_ref, pair_ref, both_ref, out_ref):
    n, rows, units = h_ref.shape
    b, c = lax.rem(at_ref[0], 2), at_ref[1]
    h = jnp.concatenate([h_ref[k] for k in range(n)], axis=1)
    parts = [
        dot_dims(h, w[...], 1, 1).astype(bf16) for w in (own_ref, other_ref, pair_ref, both_ref)
    ]
    hr = out_ref.shape[1]
    for bb in range(2):
        for cc in range(2):

            @pl.when((b == bb) & (c == cc))
            def _():
                order = [parts[2 * (p // 2 != bb) + (p % 2 != cc)] for p in range(4)]
                whole = jnp.concatenate(order, axis=1)
                for k in range(out_ref.shape[0]):
                    out_ref[k] = whole[k * hr : (k + 1) * hr]


def spread_kernel(back_ref, select_ref, out_ref):
    n, hr, feats = back_ref.shape
    rows = [
        jnp.concatenate([back_ref[2 * a], back_ref[2 * a + 1]], axis=0) for a in range(n // 2)
    ]
    whole = jnp.concatenate(rows, axis=1)
    half = out_ref.shape[2]
    for h in range(2):
        out_ref[:, h, :] = dot(select_ref[...], whole[:, h * half : (h + 1) * half]).astype(bf16)


def mix_kernel(in_ref, place_ref, out_ref):
    slots, _, half = in_ref.shape
    toks = out_ref.shape[0]
    lhs = by_half(place_ref[...].astype(f32))
    both = dot_dims(lhs, in_ref[...].reshape(2 * slots, half), 0, 0).astype(bf16)
    out_ref[:, :half] = both[:toks]
    out_ref[:, half:] = both[toks:]


def shards(tokens, node_picks, gates, gate_up, down_weight):
    group = ("y", "z")
    groups, n = lax.axis_size(group), lax.axis_size("x")
    toks, width = tokens.shape
    visits = node_picks.shape[1]
    r = toks * visits
    half = width // 2
    x = lax.axis_index("x")
    at = jnp.stack([x, lax.axis_index("core"), x // (n // 2)]).astype(i32)
    gu, dn = gate_up[0], down_weight[0].T
    feats, units = dn.shape[0], dn.shape[1] // n
    swap = [(0, 1), (1, 0)]
    pair = [(i, i ^ 1) for i in range(n)]
    send, place = call(
        pack_kernel,
        [((groups, 2, half + LANES), bf16), ((groups, toks), bf16)],
        [VMEM] * 3,
        "pack",
        room=60,
    )(node_picks.T, gates.transpose(1, 2, 0), tokens)
    dn_pair = lax.ppermute(dn, "x", pair)
    dn_pair, mine = lax.optimization_barrier((dn_pair, gu))
    gu_other = lax.ppermute(mine, "core", swap)
    dn_other = lax.ppermute(dn, "core", swap)
    arrived = lax.all_to_all(send, group, split_axis=0, concat_axis=0, tiled=True)
    arrived, dn_other = lax.optimization_barrier((arrived, dn_other))
    rows, select = call(
        compact_kernel,
        [((r, width + LANES), bf16), ((groups, r), bf16)],
        [VMEM],
        "compact",
    )(arrived)
    got = ring(rows, n)
    steps = tuple(k for k, _ in got)
    (hid,) = call(
        functools.partial(hidden_kernel, steps),
        [((n, n * r // 2, units), bf16)],
        [SMEM, HBM, HBM] + [VMEM] * n,
        "hidden",
        [pltpu.VMEM((2,) + gu.shape, bf16), pltpu.SemaphoreType.DMA((2, CHUNKS))],
        HID,
    )(at, gu, gu_other, *[b for _, b in got])
    hid, dn_pair = lax.optimization_barrier((hid, dn_pair))
    dn_both = lax.ppermute(dn_pair, "core", swap)
    hid = lax.all_to_all(hid, "x", split_axis=0, concat_axis=0, tiled=True)
    (out,) = call(
        down_kernel,
        [((n, r // 2, 4 * feats), bf16)],
        [SMEM] + [VMEM] * 5,
        "down",
        room=DOWN,
    )(at, hid, dn, dn_other, dn_pair, dn_both)
    back = lax.all_to_all(out, "x", split_axis=0, concat_axis=0, tiled=True)
    (padded,) = call(spread_kernel, [((groups, 2, half), bf16)], [VMEM] * 2, "spread")(
        back, select
    )
    returned = lax.all_to_all(padded, group, split_axis=0, concat_axis=0, tiled=True)
    (mixed,) = call(mix_kernel, [((toks, width), bf16)], [VMEM] * 2, "mix")(returned, place)
    return mixed


def solution(mesh):
    fine = Mesh(mesh.devices.reshape(8, 8, 8, 2), ("y", "z", "x", "core"))
    group, local = ("y", "z"), ("x", "core")
    every = group + local
    placed = (
        P(every, None),
        P(every, None),
        P(every, None, None),
        P(group, None, local),
        P(group, None, local),
    )
    return jax.shard_map(
        shards, mesh=fine, in_specs=placed, out_specs=P(every, None), check_vma=False
    )
```

```python
import functools

import jax
import jax.numpy as jnp
from jax import lax
from jax.experimental import pallas as pl
from jax.experimental.pallas import tpu as pltpu
from jax.sharding import Mesh
from jax.sharding import PartitionSpec as P

LANES = 128
EXPERTS = 2
bf16, f32, i32 = jnp.bfloat16, jnp.float32, jnp.int32
VMEM = pl.BlockSpec(memory_space=pltpu.VMEM)
SMEM = pl.BlockSpec(memory_space=pltpu.SMEM)
HBM = pl.BlockSpec(memory_space=pltpu.HBM)
HID = 50
DOWN = 52
CHUNKS = 4


def dot(a, b):
    return jnp.dot(a, b, preferred_element_type=f32)


def dot_dims(a, b, da, db):
    return lax.dot_general(a, b, (((da,), (db,)), ((), ())), preferred_element_type=f32)


def call(kernel, outs, specs, name, scratch=(), room=8):
    return pl.pallas_call(
        kernel,
        out_shape=[jax.ShapeDtypeStruct(s, d) for s, d in outs],
        in_specs=specs,
        out_specs=[VMEM] * len(outs),
        scratch_shapes=list(scratch),
        compiler_params=pltpu.CompilerParams(vmem_limit_bytes=room * 2**20),
        name=name,
    )


def ring(block, n):
    up = [(i, (i + 1) % n) for i in range(n)]
    down = [(i, (i - 1) % n) for i in range(n)]
    got = [(0, block)]
    fwd = back = block
    for k in range(1, n // 2):
        fwd = lax.ppermute(fwd, "x", up)
        back = lax.ppermute(back, "x", down)
        got += [(k, fwd), (n - k, back)]
    got.append((n // 2, lax.ppermute(fwd, "x", up)))
    return got


def pack_kernel(picks_ref, gates_ref, tok_ref, send_ref, place_ref):
    visits, toks = picks_ref.shape
    groups, _, wide = send_ref.shape
    half = wide - LANES
    node = lax.broadcasted_iota(i32, (groups, toks), 0)
    place = jnp.zeros((groups, toks), f32)
    lane = lax.broadcasted_iota(i32, (groups, LANES), 1)
    tail = jnp.zeros((groups, LANES), f32)
    for j in range(visits):
        hot = (node == picks_ref[j : j + 1, :]).astype(f32)
        place += hot
        for e in range(gates_ref.shape[1]):
            gate = jnp.sum(hot * gates_ref[j, e : e + 1, :].astype(f32), axis=1, keepdims=True)
            tail += jnp.where(lane == e, gate, 0.0)
    place = place.astype(bf16)
    place_ref[...] = place
    for h in range(2):
        send_ref[:, h, :half] = dot(place, tok_ref[:, h * half : (h + 1) * half]).astype(bf16)
        send_ref[:, h, half:] = tail.astype(bf16)


def by_half(hot):
    slots, k = hot.shape
    twice = jnp.broadcast_to(hot[:, None, :], (slots, 2, k)).reshape(2 * slots, k)
    parity = lax.broadcasted_iota(i32, (2 * slots, k), 0) % 2
    return jnp.concatenate([jnp.where(parity == h, twice, 0.0) for h in range(2)], axis=1).astype(
        bf16
    )


def compact_kernel(in_ref, rows_ref):
    groups, _, wide = in_ref.shape
    half = wide - LANES
    count = rows_ref.shape[0]
    tail = in_ref[:, 0, half:]
    live = (tail.astype(f32) > 0).astype(bf16)
    low = lax.broadcasted_iota(i32, (groups, groups), 0)
    high = lax.broadcasted_iota(i32, (groups, groups), 1)
    upto = dot((high <= low).astype(bf16), live)[:, :1]
    alive = live[:, :1].astype(f32) > 0
    position = lax.broadcasted_iota(i32, (groups, count), 1).astype(f32) + 1.0
    spread = jnp.where(alive & (upto == position), 1.0, 0.0)
    both = dot_dims(by_half(spread), in_ref[...].reshape(2 * groups, wide), 0, 0).astype(bf16)
    rows_ref[:, :half] = both[:count, :half]
    rows_ref[:, half : 2 * half] = both[count:, :half]
    slot = lax.broadcasted_iota(i32, (groups, count), 0).astype(f32)
    came = jnp.sum(spread * slot, axis=0, keepdims=True)
    came = jnp.broadcast_to(came, (LANES, count)).T
    lane = lax.broadcasted_iota(i32, (count, LANES), 1)
    ends = jnp.where(lane == EXPERTS, came, both[:count, half:].astype(f32))
    rows_ref[:, 2 * half :] = ends.astype(bf16)


def hidden_kernel(steps, at_ref, gu_ref, other_ref, *refs):
    blocks, (out_ref, from_ref, buf, sems) = refs[:-4], refs[-4:]
    depth = gu_ref.shape[0] // CHUNKS
    copies = []
    for i, w in enumerate((gu_ref, other_ref)):
        for k in range(CHUNKS):
            part = pl.ds(k * depth, depth)
            copies.append(
                pltpu.make_async_copy(w.at[part, :], buf.at[i, part, :], sems.at[i, k])
            )
            copies[-1].start()
    n = len(blocks)
    x, c = at_ref[0], at_ref[1]
    r = blocks[0].shape[0]
    width = gu_ref.shape[0]
    units = gu_ref.shape[1] // 2
    hr = r // 2
    rows = jnp.concatenate([b[:, :width] for b in blocks], axis=0)
    tail = jnp.concatenate([b[:, width:] for b in blocks], axis=0).astype(f32)
    gate = jnp.where(at_ref[2] == 0, tail[:, 0:1], tail[:, 1:2])
    parts = []
    for i in range(2):
        pr = 0.0
        for k in range(CHUNKS):
            copies[i * CHUNKS + k].wait()
            lo, hi = k * depth, (k + 1) * depth
            pr += dot(rows[:, lo:hi], buf[i, lo:hi, :])
        g, p = pr[:, :units], pr[:, units:]
        parts.append((g / (1.0 + jnp.exp(-g)) * p * gate).astype(bf16))
    mine, other = parts
    first = jnp.where(c == 0, mine, other)
    second = jnp.where(c == 0, other, mine)
    h = jnp.concatenate([first, second], axis=1)
    for j, k in enumerate(steps):
        owner = lax.rem(x + (n - k), n)
        at = pl.ds(pl.multiple_of(owner * hr, hr), hr)
        for dest in range(n):
            lo = j * r + (dest % 2) * hr
            out_ref[dest, at, :] = h[lo : lo + hr]
        ends = [tail[j * r + b * hr : j * r + (b + 1) * hr] for b in range(2)]
        from_ref[at, :] = jnp.where(lax.rem(x, 2) == 0, ends[0], ends[1])


def down_kernel(at_ref, h_ref, own_ref, other_ref, pair_ref, both_ref, ends_ref, out_ref, whole):
    n, rows, units = h_ref.shape
    b, c = lax.rem(at_ref[0], 2), at_ref[1]
    h = jnp.concatenate([h_ref[k] for k in range(n)], axis=1)
    parts = [
        dot_dims(h, w[...], 1, 1).astype(bf16) for w in (own_ref, other_ref, pair_ref, both_ref)
    ]
    for bb in range(2):
        for cc in range(2):

            @pl.when((b == bb) & (c == cc))
            def _():
                order = [parts[2 * (p // 2 != bb) + (p % 2 != cc)] for p in range(4)]
                whole[...] = jnp.concatenate(order, axis=1)

    slots, half = out_ref.shape[0], whole.shape[1] // 2
    group = ends_ref[...].T[EXPERTS : EXPERTS + 1, :].astype(i32)
    owner = lax.broadcasted_iota(i32, (1, rows), 1) // (rows // n)
    slot = lax.broadcasted_iota(i32, (slots, rows), 0)
    place = (slot == group * n + owner).astype(f32).astype(bf16)
    for k in range(2):
        out_ref[:, k, :half] = dot(place, whole[:, k * half : (k + 1) * half]).astype(bf16)


def mix_kernel(in_ref, place_ref, out_ref):
    slots = in_ref.shape[0]
    groups, toks = place_ref.shape
    n = slots // groups
    half = out_ref.shape[1] // n
    spread = jnp.broadcast_to(place_ref[...].astype(f32)[:, None, :], (groups, 2 * n, toks))
    spread = spread.reshape(2 * slots, toks)
    row = lax.broadcasted_iota(i32, (2 * slots, toks), 0)
    which = (row % (2 * n)) // 4 * 2 + row % 2
    lhs = jnp.concatenate([jnp.where(which == q, spread, 0.0) for q in range(n)], axis=1)
    flat = in_ref[...].reshape(2 * slots, in_ref.shape[2])
    both = dot_dims(lhs.astype(bf16), flat, 0, 0).astype(bf16)
    out_ref[...] = jnp.concatenate(
        [both[q * toks : (q + 1) * toks, :half] for q in range(n)], axis=1
    )


def shards(tokens, node_picks, gates, gate_up, down_weight):
    group = ("y", "z")
    groups, n = lax.axis_size(group), lax.axis_size("x")
    toks, width = tokens.shape
    visits = node_picks.shape[1]
    r = toks * visits
    half = width // 2
    x = lax.axis_index("x")
    at = jnp.stack([x, lax.axis_index("core"), x // (n // 2)]).astype(i32)
    gu, dn = gate_up[0], down_weight[0].T
    feats, units = dn.shape[0], dn.shape[1] // n
    swap = [(0, 1), (1, 0)]
    pair = [(i, i ^ 1) for i in range(n)]
    send, place = call(
        pack_kernel,
        [((groups, 2, half + LANES), bf16), ((groups, toks), bf16)],
        [VMEM] * 3,
        "pack",
        room=60,
    )(node_picks.T, gates.transpose(1, 2, 0), tokens)
    dn_pair = lax.ppermute(dn, "x", pair)
    dn_pair, mine = lax.optimization_barrier((dn_pair, gu))
    gu_other = lax.ppermute(mine, "core", swap)
    dn_other = lax.ppermute(dn, "core", swap)
    arrived = lax.all_to_all(send, group, split_axis=0, concat_axis=0, tiled=True)
    arrived, dn_other = lax.optimization_barrier((arrived, dn_other))
    (rows,) = call(
        compact_kernel,
        [((r, width + LANES), bf16)],
        [VMEM],
        "compact",
    )(arrived)
    got = ring(rows, n)
    steps = tuple(k for k, _ in got)
    hid, ends = call(
        functools.partial(hidden_kernel, steps),
        [((n, n * r // 2, units), bf16), ((n * r // 2, LANES), f32)],
        [SMEM, HBM, HBM] + [VMEM] * n,
        "hidden",
        [pltpu.VMEM((2,) + gu.shape, bf16), pltpu.SemaphoreType.DMA((2, CHUNKS))],
        HID,
    )(at, gu, gu_other, *[b for _, b in got])
    hid, dn_pair = lax.optimization_barrier((hid, dn_pair))
    dn_both = lax.ppermute(dn_pair, "core", swap)
    hid = lax.all_to_all(hid, "x", split_axis=0, concat_axis=0, tiled=True)
    lanes = -(-2 * feats // LANES) * LANES
    (out,) = call(
        down_kernel,
        [((groups * n, 2, lanes), bf16)],
        [SMEM] + [VMEM] * 6,
        "down",
        [pltpu.VMEM((n * r // 2, 4 * feats), bf16)],
        DOWN,
    )(at, hid, dn, dn_other, dn_pair, dn_both, ends)
    returned = lax.all_to_all(out, group + ("x",), split_axis=0, concat_axis=0, tiled=True)
    (mixed,) = call(mix_kernel, [((toks, width), bf16)], [VMEM] * 2, "mix")(returned, place)
    return mixed


def solution(mesh):
    fine = Mesh(mesh.devices.reshape(8, 8, 8, 2), ("y", "z", "x", "core"))
    group, local = ("y", "z"), ("x", "core")
    every = group + local
    placed = (
        P(every, None),
        P(every, None),
        P(every, None, None),
        P(group, None, local),
        P(group, None, local),
    )
    return jax.shard_map(
        shards, mesh=fine, in_specs=placed, out_specs=P(every, None), check_vma=False
    )
```

```python
import functools

import jax
import jax.numpy as jnp
from jax import lax
from jax.experimental import pallas as pl
from jax.experimental.pallas import tpu as pltpu
from jax.sharding import Mesh
from jax.sharding import PartitionSpec as P

LANES = 128
bf16, f32, i32 = jnp.bfloat16, jnp.float32, jnp.int32
VMEM = pl.BlockSpec(memory_space=pltpu.VMEM)
SMEM = pl.BlockSpec(memory_space=pltpu.SMEM)
HBM = pl.BlockSpec(memory_space=pltpu.HBM)
HID = 50
DOWN = 52
CHUNKS = 4


def dot(a, b):
    return jnp.dot(a, b, preferred_element_type=f32)


def dot_dims(a, b, da, db):
    return lax.dot_general(a, b, (((da,), (db,)), ((), ())), preferred_element_type=f32)


def call(kernel, outs, specs, name, scratch=(), room=8):
    return pl.pallas_call(
        kernel,
        out_shape=[jax.ShapeDtypeStruct(s, d) for s, d in outs],
        in_specs=specs,
        out_specs=[VMEM] * len(outs),
        scratch_shapes=list(scratch),
        compiler_params=pltpu.CompilerParams(vmem_limit_bytes=room * 2**20),
        name=name,
    )


def ring(block, n):
    up = [(i, (i + 1) % n) for i in range(n)]
    down = [(i, (i - 1) % n) for i in range(n)]
    got = [(0, block)]
    fwd = back = block
    for k in range(1, n // 2):
        fwd = lax.ppermute(fwd, "x", up)
        back = lax.ppermute(back, "x", down)
        got += [(k, fwd), (n - k, back)]
    got.append((n // 2, lax.ppermute(fwd, "x", up)))
    return got


def pack_kernel(*refs):
    sources, (send_ref, place_ref), held, sems = refs[:3], refs[3:5], refs[5:8], refs[8]
    copies = [pltpu.make_async_copy(sources[i], held[i], sems.at[i]) for i in range(3)]
    for copy in copies:
        copy.start()
    picks_ref, gates_ref, tok_ref = held
    copies[0].wait()
    copies[1].wait()
    visits, toks = picks_ref.shape
    groups, _, wide = send_ref.shape
    half = wide - LANES
    node = lax.broadcasted_iota(i32, (groups, toks), 0)
    place = jnp.zeros((groups, toks), f32)
    lane = lax.broadcasted_iota(i32, (groups, LANES), 1)
    tail = jnp.zeros((groups, LANES), f32)
    for j in range(visits):
        hot = (node == picks_ref[j : j + 1, :]).astype(f32)
        place += hot
        for e in range(gates_ref.shape[1]):
            gate = jnp.sum(hot * gates_ref[j, e : e + 1, :].astype(f32), axis=1, keepdims=True)
            tail += jnp.where(lane == e, gate, 0.0)
    place = place.astype(bf16)
    place_ref[...] = place
    copies[2].wait()
    for h in range(2):
        send_ref[:, h, :half] = dot(place, tok_ref[:, h * half : (h + 1) * half]).astype(bf16)
        send_ref[:, h, half:] = tail.astype(bf16)


def by_half(hot):
    slots, k = hot.shape
    twice = jnp.broadcast_to(hot[:, None, :], (slots, 2, k)).reshape(2 * slots, k)
    parity = lax.broadcasted_iota(i32, (2 * slots, k), 0) % 2
    return jnp.concatenate([jnp.where(parity == h, twice, 0.0) for h in range(2)], axis=1).astype(
        bf16
    )


def compact_kernel(in_ref, rows_ref, select_ref):
    groups, _, wide = in_ref.shape
    half = wide - LANES
    count = rows_ref.shape[0]
    tail = in_ref[:, 0, half:]
    live = (tail.astype(f32) > 0).astype(bf16)
    low = lax.broadcasted_iota(i32, (groups, groups), 0)
    high = lax.broadcasted_iota(i32, (groups, groups), 1)
    upto = dot((high <= low).astype(bf16), live)[:, :1]
    alive = live[:, :1].astype(f32) > 0
    position = lax.broadcasted_iota(i32, (groups, count), 1).astype(f32) + 1.0
    spread = jnp.where(alive & (upto == position), 1.0, 0.0)
    select_ref[...] = spread.astype(bf16)
    both = dot_dims(by_half(spread), in_ref[...].reshape(2 * groups, wide), 0, 0).astype(bf16)
    rows_ref[:, :half] = both[:count, :half]
    rows_ref[:, half : 2 * half] = both[count:, :half]
    rows_ref[:, 2 * half :] = both[:count, half:]


def hidden_kernel(steps, at_ref, gu_ref, other_ref, *refs):
    blocks, (out_ref, buf, sems, late, late_sem) = refs[:-5], refs[-5:]
    last = pltpu.make_async_copy(blocks[-1], late, late_sem)
    last.start()
    blocks = blocks[:-1] + (late,)
    depth = gu_ref.shape[0] // CHUNKS
    copies = []
    for i, w in enumerate((gu_ref, other_ref)):
        for k in range(CHUNKS):
            part = pl.ds(k * depth, depth)
            copies.append(
                pltpu.make_async_copy(w.at[part, :], buf.at[i, part, :], sems.at[i, k])
            )
            copies[-1].start()
    n = len(blocks)
    x, c = at_ref[0], at_ref[1]
    r = blocks[0].shape[0]
    width = gu_ref.shape[0]
    units = gu_ref.shape[1] // 2
    hr = r // 2
    last.wait()
    rows = jnp.concatenate([b[:, :width] for b in blocks], axis=0)
    tail = jnp.concatenate([b[:, width:] for b in blocks], axis=0).astype(f32)
    gate = jnp.where(at_ref[2] == 0, tail[:, 0:1], tail[:, 1:2])
    parts = []
    for i in range(2):
        pr = 0.0
        for k in range(CHUNKS):
            copies[i * CHUNKS + k].wait()
            lo, hi = k * depth, (k + 1) * depth
            pr += dot(rows[:, lo:hi], buf[i, lo:hi, :])
        g, p = pr[:, :units], pr[:, units:]
        parts.append((g / (1.0 + jnp.exp(-g)) * p * gate).astype(bf16))
    mine, other = parts
    first = jnp.where(c == 0, mine, other)
    second = jnp.where(c == 0, other, mine)
    h = jnp.concatenate([first, second], axis=1)
    for j, k in enumerate(steps):
        owner = lax.rem(x + (n - k), n)
        at = pl.ds(pl.multiple_of(owner * hr, hr), hr)
        for dest in range(n):
            lo = j * r + (dest % 2) * hr
            out_ref[dest, at, :] = h[lo : lo + hr]


def down_kernel(at_ref, h_ref, own_ref, other_ref, pair_ref, both_ref, out_ref):
    n, rows, units = h_ref.shape
    b, c = lax.rem(at_ref[0], 2), at_ref[1]
    h = jnp.concatenate([h_ref[k] for k in range(n)], axis=1)
    parts = [
        dot_dims(h, w[...], 1, 1).astype(bf16) for w in (own_ref, other_ref, pair_ref, both_ref)
    ]
    hr = out_ref.shape[1]
    for bb in range(2):
        for cc in range(2):

            @pl.when((b == bb) & (c == cc))
            def _():
                order = [parts[2 * (p // 2 != bb) + (p % 2 != cc)] for p in range(4)]
                whole = jnp.concatenate(order, axis=1)
                for k in range(out_ref.shape[0]):
                    out_ref[k] = whole[k * hr : (k + 1) * hr]


def spread_kernel(back_ref, select_ref, out_ref):
    n, hr, feats = back_ref.shape
    rows = [
        jnp.concatenate([back_ref[2 * a], back_ref[2 * a + 1]], axis=0) for a in range(n // 2)
    ]
    whole = jnp.concatenate(rows, axis=1)
    half = out_ref.shape[2]
    for h in range(2):
        out_ref[:, h, :] = dot(select_ref[...], whole[:, h * half : (h + 1) * half]).astype(bf16)


def mix_kernel(in_ref, place_ref, out_ref):
    slots, _, half = in_ref.shape
    toks = out_ref.shape[0]
    lhs = by_half(place_ref[...].astype(f32))
    both = dot_dims(lhs, in_ref[...].reshape(2 * slots, half), 0, 0).astype(bf16)
    out_ref[:, :half] = both[:toks]
    out_ref[:, half:] = both[toks:]


def shards(tokens, node_picks, gates, gate_up, down_weight):
    group = ("y", "z")
    groups, n = lax.axis_size(group), lax.axis_size("x")
    toks, width = tokens.shape
    visits = node_picks.shape[1]
    r = toks * visits
    half = width // 2
    x = lax.axis_index("x")
    at = jnp.stack([x, lax.axis_index("core"), x // (n // 2)]).astype(i32)
    gu, dn = gate_up[0], down_weight[0].T
    feats, units = dn.shape[0], dn.shape[1] // n
    swap = [(0, 1), (1, 0)]
    pair = [(i, i ^ 1) for i in range(n)]
    asked = (node_picks.T, gates.transpose(1, 2, 0), tokens)
    send, place = call(
        pack_kernel,
        [((groups, 2, half + LANES), bf16), ((groups, toks), bf16)],
        [HBM] * 3,
        "pack",
        [pltpu.VMEM(a.shape, a.dtype) for a in asked] + [pltpu.SemaphoreType.DMA((3,))],
        60,
    )(*asked)
    dn_pair = lax.ppermute(dn, "x", pair)
    dn_pair, mine = lax.optimization_barrier((dn_pair, gu))
    gu_other = lax.ppermute(mine, "core", swap)
    dn_other = lax.ppermute(dn, "core", swap)
    arrived = lax.all_to_all(send, group, split_axis=0, concat_axis=0, tiled=True)
    arrived, dn_other = lax.optimization_barrier((arrived, dn_other))
    rows, select = call(
        compact_kernel,
        [((r, width + LANES), bf16), ((groups, r), bf16)],
        [VMEM],
        "compact",
    )(arrived)
    got = ring(rows, n)
    steps = tuple(k for k, _ in got)
    (hid,) = call(
        functools.partial(hidden_kernel, steps),
        [((n, n * r // 2, units), bf16)],
        [SMEM, HBM, HBM] + [VMEM] * (n - 1) + [HBM],
        "hidden",
        [pltpu.VMEM((2,) + gu.shape, bf16), pltpu.SemaphoreType.DMA((2, CHUNKS))]
        + [pltpu.VMEM(rows.shape, bf16), pltpu.SemaphoreType.DMA],
        HID,
    )(at, gu, gu_other, *[b for _, b in got])
    dn_both = lax.ppermute(dn_pair, "core", swap)
    hid = lax.all_to_all(hid, "x", split_axis=0, concat_axis=0, tiled=True)
    (out,) = call(
        down_kernel,
        [((n, r // 2, 4 * feats), bf16)],
        [SMEM] + [VMEM] * 5,
        "down",
        room=DOWN,
    )(at, hid, dn, dn_other, dn_pair, dn_both)
    back = lax.all_to_all(out, "x", split_axis=0, concat_axis=0, tiled=True)
    (padded,) = call(spread_kernel, [((groups, 2, half), bf16)], [VMEM] * 2, "spread")(
        back, select
    )
    returned = lax.all_to_all(padded, group, split_axis=0, concat_axis=0, tiled=True)
    (mixed,) = call(mix_kernel, [((toks, width), bf16)], [VMEM] * 2, "mix")(returned, place)
    return mixed


def solution(mesh):
    fine = Mesh(mesh.devices.reshape(8, 8, 8, 2), ("y", "z", "x", "core"))
    group, local = ("y", "z"), ("x", "core")
    every = group + local
    placed = (
        P(every, None),
        P(every, None),
        P(every, None, None),
        P(group, None, local),
        P(group, None, local),
    )
    return jax.shard_map(
        shards, mesh=fine, in_specs=placed, out_specs=P(every, None), check_vma=False
    )
```

```python
import functools

import jax
import jax.numpy as jnp
from jax import lax
from jax.experimental import pallas as pl
from jax.experimental.pallas import tpu as pltpu
from jax.sharding import Mesh
from jax.sharding import PartitionSpec as P

LANES = 128
bf16, f32, i32 = jnp.bfloat16, jnp.float32, jnp.int32
VMEM = pl.BlockSpec(memory_space=pltpu.VMEM)
SMEM = pl.BlockSpec(memory_space=pltpu.SMEM)
HBM = pl.BlockSpec(memory_space=pltpu.HBM)
HID = 50
DOWN = 52
CHUNKS = 4


COSTS = {"compact": pl.CostEstimate(flops=10**10, bytes_accessed=2**24, transcendentals=0)}


def dot(a, b):
    return jnp.dot(a, b, preferred_element_type=f32)


def dot_dims(a, b, da, db):
    return lax.dot_general(a, b, (((da,), (db,)), ((), ())), preferred_element_type=f32)


def call(kernel, outs, specs, name, scratch=(), room=8):
    return pl.pallas_call(
        kernel,
        out_shape=[jax.ShapeDtypeStruct(s, d) for s, d in outs],
        in_specs=specs,
        out_specs=[VMEM] * len(outs),
        scratch_shapes=list(scratch),
        cost_estimate=COSTS.get(name),
        compiler_params=pltpu.CompilerParams(vmem_limit_bytes=room * 2**20),
        name=name,
    )


def ring(block, n):
    up = [(i, (i + 1) % n) for i in range(n)]
    down = [(i, (i - 1) % n) for i in range(n)]
    got = [(0, block)]
    fwd = back = near = block
    for k in range(1, n // 2):
        near = back
        fwd = lax.ppermute(fwd, "x", up)
        back = lax.ppermute(back, "x", down)
        got += [(k, fwd), (n - k, back)]
    twice = [(i, (i - 2) % n) for i in range(n)]
    got.append((n // 2, lax.ppermute(near, "x", twice)))
    return got


def pack_kernel(*refs):
    sources, (send_ref, place_ref), held, sems = refs[:3], refs[3:5], refs[5:8], refs[8]
    copies = [pltpu.make_async_copy(sources[i], held[i], sems.at[i]) for i in range(3)]
    for copy in copies:
        copy.start()
    picks_ref, gates_ref, tok_ref = held
    copies[0].wait()
    copies[1].wait()
    visits, toks = picks_ref.shape
    groups, _, wide = send_ref.shape
    half = wide - LANES
    node = lax.broadcasted_iota(i32, (groups, toks), 0)
    place = jnp.zeros((groups, toks), f32)
    lane = lax.broadcasted_iota(i32, (groups, LANES), 1)
    tail = jnp.zeros((groups, LANES), f32)
    for j in range(visits):
        hot = (node == picks_ref[j : j + 1, :]).astype(f32)
        place += hot
        for e in range(gates_ref.shape[1]):
            gate = jnp.sum(hot * gates_ref[j, e : e + 1, :].astype(f32), axis=1, keepdims=True)
            tail += jnp.where(lane == e, gate, 0.0)
    place = place.astype(bf16)
    place_ref[...] = place
    copies[2].wait()
    for h in range(2):
        send_ref[:, h, :half] = dot(place, tok_ref[:, h * half : (h + 1) * half]).astype(bf16)
        send_ref[:, h, half:] = tail.astype(bf16)


def by_half(hot):
    slots, k = hot.shape
    twice = jnp.broadcast_to(hot[:, None, :], (slots, 2, k)).reshape(2 * slots, k)
    parity = lax.broadcasted_iota(i32, (2 * slots, k), 0) % 2
    return jnp.concatenate([jnp.where(parity == h, twice, 0.0) for h in range(2)], axis=1).astype(
        bf16
    )


def compact_kernel(in_ref, rows_ref, select_ref):
    groups, _, wide = in_ref.shape
    half = wide - LANES
    count = rows_ref.shape[0]
    tail = in_ref[:, 0, half:]
    live = (tail.astype(f32) > 0).astype(bf16)
    low = lax.broadcasted_iota(i32, (groups, groups), 0)
    high = lax.broadcasted_iota(i32, (groups, groups), 1)
    upto = dot((high <= low).astype(bf16), live)[:, :1]
    alive = live[:, :1].astype(f32) > 0
    position = lax.broadcasted_iota(i32, (groups, count), 1).astype(f32) + 1.0
    spread = jnp.where(alive & (upto == position), 1.0, 0.0)
    select_ref[...] = spread.astype(bf16)
    both = dot_dims(by_half(spread), in_ref[...].reshape(2 * groups, wide), 0, 0).astype(bf16)
    rows_ref[:, :half] = both[:count, :half]
    rows_ref[:, half : 2 * half] = both[count:, :half]
    rows_ref[:, 2 * half :] = both[:count, half:]


def hidden_kernel(steps, at_ref, gu_ref, other_ref, *refs):
    blocks, (out_ref, buf, sems) = refs[:-3], refs[-3:]
    depth = gu_ref.shape[0] // CHUNKS
    copies = []
    for i, w in enumerate((gu_ref, other_ref)):
        for k in range(CHUNKS):
            part = pl.ds(k * depth, depth)
            copies.append(
                pltpu.make_async_copy(w.at[part, :], buf.at[i, part, :], sems.at[i, k])
            )
            copies[-1].start()
    n = len(blocks)
    x, c = at_ref[0], at_ref[1]
    r = blocks[0].shape[0]
    width = gu_ref.shape[0]
    units = gu_ref.shape[1] // 2
    hr = r // 2
    rows = jnp.concatenate([b[:, :width] for b in blocks], axis=0)
    tail = jnp.concatenate([b[:, width:] for b in blocks], axis=0).astype(f32)
    gate = jnp.where(at_ref[2] == 0, tail[:, 0:1], tail[:, 1:2])
    parts = []
    for i in range(2):
        pr = 0.0
        for k in range(CHUNKS):
            copies[i * CHUNKS + k].wait()
            lo, hi = k * depth, (k + 1) * depth
            pr += dot(rows[:, lo:hi], buf[i, lo:hi, :])
        g, p = pr[:, :units], pr[:, units:]
        parts.append((g / (1.0 + jnp.exp(-g)) * p * gate).astype(bf16))
    mine, other = parts
    first = jnp.where(c == 0, mine, other)
    second = jnp.where(c == 0, other, mine)
    h = jnp.concatenate([first, second], axis=1)
    for j, k in enumerate(steps):
        owner = lax.rem(x + (n - k), n)
        at = pl.ds(pl.multiple_of(owner * hr, hr), hr)
        for dest in range(n):
            lo = j * r + (dest % 2) * hr
            out_ref[dest, at, :] = h[lo : lo + hr]


def down_kernel(at_ref, h_ref, own_ref, other_ref, pair_ref, both_ref, out_ref):
    n, rows, units = h_ref.shape
    b, c = lax.rem(at_ref[0], 2), at_ref[1]
    h = jnp.concatenate([h_ref[k] for k in range(n)], axis=1)
    parts = [
        dot_dims(h, w[...], 1, 1).astype(bf16) for w in (own_ref, other_ref, pair_ref, both_ref)
    ]
    hr = out_ref.shape[1]
    for bb in range(2):
        for cc in range(2):

            @pl.when((b == bb) & (c == cc))
            def _():
                order = [parts[2 * (p // 2 != bb) + (p % 2 != cc)] for p in range(4)]
                whole = jnp.concatenate(order, axis=1)
                for k in range(out_ref.shape[0]):
                    out_ref[k] = whole[k * hr : (k + 1) * hr]


def spread_kernel(back_ref, select_ref, out_ref):
    n, hr, feats = back_ref.shape
    rows = [
        jnp.concatenate([back_ref[2 * a], back_ref[2 * a + 1]], axis=0) for a in range(n // 2)
    ]
    whole = jnp.concatenate(rows, axis=1)
    half = out_ref.shape[2]
    for h in range(2):
        out_ref[:, h, :] = dot(select_ref[...], whole[:, h * half : (h + 1) * half]).astype(bf16)


def mix_kernel(in_ref, place_ref, out_ref):
    slots, _, half = in_ref.shape
    toks = out_ref.shape[0]
    lhs = by_half(place_ref[...].astype(f32))
    both = dot_dims(lhs, in_ref[...].reshape(2 * slots, half), 0, 0).astype(bf16)
    out_ref[:, :half] = both[:toks]
    out_ref[:, half:] = both[toks:]


def shards(tokens, node_picks, gates, gate_up, down_weight):
    group = ("y", "z")
    groups, n = lax.axis_size(group), lax.axis_size("x")
    toks, width = tokens.shape
    visits = node_picks.shape[1]
    r = toks * visits
    half = width // 2
    x = lax.axis_index("x")
    at = jnp.stack([x, lax.axis_index("core"), x // (n // 2)]).astype(i32)
    gu, dn = gate_up[0], down_weight[0].T
    feats, units = dn.shape[0], dn.shape[1] // n
    swap = [(0, 1), (1, 0)]
    pair = [(i, i ^ 1) for i in range(n)]
    asked = (node_picks.T, gates.transpose(1, 2, 0), tokens)
    send, place = call(
        pack_kernel,
        [((groups, 2, half + LANES), bf16), ((groups, toks), bf16)],
        [HBM] * 3,
        "pack",
        [pltpu.VMEM(a.shape, a.dtype) for a in asked] + [pltpu.SemaphoreType.DMA((3,))],
        60,
    )(*asked)
    dn_pair = lax.ppermute(dn, "x", pair)
    dn_pair, mine = lax.optimization_barrier((dn_pair, gu))
    gu_other = lax.ppermute(mine, "core", swap)
    dn_other = lax.ppermute(dn, "core", swap)
    arrived = lax.all_to_all(send, group, split_axis=0, concat_axis=0, tiled=True)
    arrived, dn_other = lax.optimization_barrier((arrived, dn_other))
    rows, select = call(
        compact_kernel,
        [((r, width + LANES), bf16), ((groups, r), bf16)],
        [VMEM],
        "compact",
    )(arrived)
    got = ring(rows, n)
    steps = tuple(k for k, _ in got)
    (hid,) = call(
        functools.partial(hidden_kernel, steps),
        [((n, n * r // 2, units), bf16)],
        [SMEM, HBM, HBM] + [VMEM] * n,
        "hidden",
        [pltpu.VMEM((2,) + gu.shape, bf16), pltpu.SemaphoreType.DMA((2, CHUNKS))],
        HID,
    )(at, gu, gu_other, *[b for _, b in got])
    dn_both = lax.ppermute(dn_pair, "core", swap)
    hid = lax.all_to_all(hid, "x", split_axis=0, concat_axis=0, tiled=True)
    (out,) = call(
        down_kernel,
        [((n, r // 2, 4 * feats), bf16)],
        [SMEM] + [VMEM] * 5,
        "down",
        room=DOWN,
    )(at, hid, dn, dn_other, dn_pair, dn_both)
    back = lax.all_to_all(out, "x", split_axis=0, concat_axis=0, tiled=True)
    (padded,) = call(spread_kernel, [((groups, 2, half), bf16)], [VMEM] * 2, "spread")(
        back, select
    )
    returned = lax.all_to_all(padded, group, split_axis=0, concat_axis=0, tiled=True)
    (mixed,) = call(mix_kernel, [((toks, width), bf16)], [VMEM] * 2, "mix")(returned, place)
    return mixed


def solution(mesh):
    fine = Mesh(mesh.devices.reshape(8, 8, 8, 2), ("y", "z", "x", "core"))
    group, local = ("y", "z"), ("x", "core")
    every = group + local
    placed = (
        P(every, None),
        P(every, None),
        P(every, None, None),
        P(group, None, local),
        P(group, None, local),
    )
    return jax.shard_map(
        shards, mesh=fine, in_specs=placed, out_specs=P(every, None), check_vma=False
    )
```

```python
import functools

import jax
import jax.numpy as jnp
from jax import lax
from jax.experimental import pallas as pl
from jax.experimental.pallas import tpu as pltpu
from jax.sharding import Mesh
from jax.sharding import PartitionSpec as P

LANES = 128
bf16, f32, i32 = jnp.bfloat16, jnp.float32, jnp.int32
VMEM = pl.BlockSpec(memory_space=pltpu.VMEM)
SMEM = pl.BlockSpec(memory_space=pltpu.SMEM)
HBM = pl.BlockSpec(memory_space=pltpu.HBM)
HID = 50
DOWN = 52
CHUNKS = 4


COSTS = {"compact": pl.CostEstimate(flops=10**10, bytes_accessed=2**24, transcendentals=0)}


def dot(a, b):
    return jnp.dot(a, b, preferred_element_type=f32)


def dot_dims(a, b, da, db):
    return lax.dot_general(a, b, (((da,), (db,)), ((), ())), preferred_element_type=f32)


def call(kernel, outs, specs, name, scratch=(), room=8):
    return pl.pallas_call(
        kernel,
        out_shape=[jax.ShapeDtypeStruct(s, d) for s, d in outs],
        in_specs=specs,
        out_specs=[VMEM] * len(outs),
        scratch_shapes=list(scratch),
        cost_estimate=COSTS.get(name),
        compiler_params=pltpu.CompilerParams(vmem_limit_bytes=room * 2**20),
        name=name,
    )


def ring(block, n):
    up = [(i, (i + 1) % n) for i in range(n)]
    down = [(i, (i - 1) % n) for i in range(n)]
    got = [(0, block)]
    fwd = back = near = block
    for k in range(1, n // 2):
        near = back
        fwd = lax.ppermute(fwd, "x", up)
        back = lax.ppermute(back, "x", down)
        got += [(k, fwd), (n - k, back)]
    twice = [(i, (i - 2) % n) for i in range(n)]
    got.append((n // 2, lax.ppermute(near, "x", twice)))
    return got


def pack_kernel(*refs):
    sources, (send_ref, place_ref), held, sems = refs[:3], refs[3:5], refs[5:8], refs[8]
    copies = [pltpu.make_async_copy(sources[i], held[i], sems.at[i]) for i in range(3)]
    for copy in copies:
        copy.start()
    picks_ref, gates_ref, tok_ref = held
    copies[0].wait()
    copies[1].wait()
    visits, toks = picks_ref.shape
    groups, _, wide = send_ref.shape
    half = wide - LANES
    node = lax.broadcasted_iota(i32, (groups, toks), 0)
    place = jnp.zeros((groups, toks), f32)
    lane = lax.broadcasted_iota(i32, (groups, LANES), 1)
    tail = jnp.zeros((groups, LANES), f32)
    for j in range(visits):
        hot = (node == picks_ref[j : j + 1, :]).astype(f32)
        place += hot
        for e in range(gates_ref.shape[1]):
            gate = jnp.sum(hot * gates_ref[j, e : e + 1, :].astype(f32), axis=1, keepdims=True)
            tail += jnp.where(lane == e, gate, 0.0)
    place = place.astype(bf16)
    place_ref[...] = place
    copies[2].wait()
    for h in range(2):
        send_ref[:, h, :half] = dot(place, tok_ref[:, h * half : (h + 1) * half]).astype(bf16)
        send_ref[:, h, half:] = tail.astype(bf16)


def by_half(hot):
    slots, k = hot.shape
    twice = jnp.broadcast_to(hot[:, None, :], (slots, 2, k)).reshape(2 * slots, k)
    parity = lax.broadcasted_iota(i32, (2 * slots, k), 0) % 2
    return jnp.concatenate([jnp.where(parity == h, twice, 0.0) for h in range(2)], axis=1).astype(
        bf16
    )


def compact_kernel(in_ref, rows_ref, select_ref):
    groups, _, wide = in_ref.shape
    half = wide - LANES
    count = rows_ref.shape[0]
    tail = in_ref[:, 0, half:]
    live = (tail.astype(f32) > 0).astype(bf16)
    low = lax.broadcasted_iota(i32, (groups, groups), 0)
    high = lax.broadcasted_iota(i32, (groups, groups), 1)
    upto = dot((high <= low).astype(bf16), live)[:, :1]
    alive = live[:, :1].astype(f32) > 0
    position = lax.broadcasted_iota(i32, (groups, count), 1).astype(f32) + 1.0
    spread = jnp.where(alive & (upto == position), 1.0, 0.0)
    select_ref[...] = spread.astype(bf16)
    both = dot_dims(by_half(spread), in_ref[...].reshape(2 * groups, wide), 0, 0).astype(bf16)
    rows_ref[:, :half] = both[:count, :half]
    rows_ref[:, half : 2 * half] = both[count:, :half]
    rows_ref[:, 2 * half :] = both[:count, half:]


def hidden_kernel(steps, at_ref, gu_ref, other_ref, *refs):
    blocks, (out_ref, buf, sems) = refs[:-3], refs[-3:]
    depth = gu_ref.shape[0] // CHUNKS
    copies = []
    for i, w in enumerate((gu_ref, other_ref)):
        for k in range(CHUNKS):
            part = pl.ds(k * depth, depth)
            copies.append(
                pltpu.make_async_copy(w.at[part, :], buf.at[i, part, :], sems.at[i, k])
            )
            copies[-1].start()
    n = len(blocks)
    x, c = at_ref[0], at_ref[1]
    r = blocks[0].shape[0]
    width = gu_ref.shape[0]
    units = gu_ref.shape[1] // 2
    hr = r // 2
    rows = jnp.concatenate([b[:, :width] for b in blocks], axis=0)
    tail = jnp.concatenate([b[:, width:] for b in blocks], axis=0).astype(f32)
    gate = jnp.where(at_ref[2] == 0, tail[:, 0:1], tail[:, 1:2])
    parts = []
    for i in range(2):
        pr = 0.0
        for k in range(CHUNKS):
            copies[i * CHUNKS + k].wait()
            lo, hi = k * depth, (k + 1) * depth
            pr += dot(rows[:, lo:hi], buf[i, lo:hi, :])
        g, p = pr[:, :units], pr[:, units:]
        parts.append((g / (1.0 + jnp.exp(-g)) * p * gate).astype(bf16))
    mine, other = parts
    first = jnp.where(c == 0, mine, other)
    second = jnp.where(c == 0, other, mine)
    h = jnp.concatenate([first, second], axis=1)
    for j, k in enumerate(steps):
        owner = lax.rem(x + (n - k), n)
        at = pl.ds(pl.multiple_of(owner * hr, hr), hr)
        for dest in range(n):
            lo = j * r + (dest % 2) * hr
            out_ref[dest, at, :] = h[lo : lo + hr]


def down_kernel(at_ref, h_ref, own_ref, other_ref, pair_ref, both_ref, out_ref):
    n, rows, units = h_ref.shape
    b, c = lax.rem(at_ref[0], 2), at_ref[1]
    h = jnp.concatenate([h_ref[k] for k in range(n)], axis=1)
    parts = [
        dot_dims(h, w[...], 1, 1).astype(bf16) for w in (own_ref, other_ref, pair_ref, both_ref)
    ]
    hr = out_ref.shape[1]
    for bb in range(2):
        for cc in range(2):

            @pl.when((b == bb) & (c == cc))
            def _():
                order = [parts[2 * (p // 2 != bb) + (p % 2 != cc)] for p in range(4)]
                whole = jnp.concatenate(order, axis=1)
                for k in range(out_ref.shape[0]):
                    out_ref[k] = whole[k * hr : (k + 1) * hr]


def spread_kernel(back_ref, select_ref, out_ref):
    n, hr, feats = back_ref.shape
    rows = [
        jnp.concatenate([back_ref[2 * a], back_ref[2 * a + 1]], axis=0) for a in range(n // 2)
    ]
    whole = jnp.concatenate(rows, axis=1)
    half = out_ref.shape[2]
    for h in range(2):
        out_ref[:, h, :] = dot(select_ref[...], whole[:, h * half : (h + 1) * half]).astype(bf16)


def mix_kernel(in_ref, place_ref, out_ref):
    slots, _, half = in_ref.shape
    toks = out_ref.shape[0]
    lhs = by_half(place_ref[...].astype(f32))
    both = dot_dims(lhs, in_ref[...].reshape(2 * slots, half), 0, 0).astype(bf16)
    out_ref[:, :half] = both[:toks]
    out_ref[:, half:] = both[toks:]


def shards(tokens, node_picks, gates, gate_up, down_weight):
    group = ("y", "z")
    groups, n = lax.axis_size(group), lax.axis_size("x")
    toks, width = tokens.shape
    visits = node_picks.shape[1]
    r = toks * visits
    half = width // 2
    x = lax.axis_index("x")
    at = jnp.stack([x, lax.axis_index("core"), x // (n // 2)]).astype(i32)
    gu, dn = gate_up[0], down_weight[0].T
    feats, units = dn.shape[0], dn.shape[1] // n
    swap = [(0, 1), (1, 0)]
    pair = [(i, i ^ 1) for i in range(n)]
    asked = (node_picks.T, gates.transpose(1, 2, 0), tokens)
    send, place = call(
        pack_kernel,
        [((groups, 2, half + LANES), bf16), ((groups, toks), bf16)],
        [HBM] * 3,
        "pack",
        [pltpu.VMEM(a.shape, a.dtype) for a in asked] + [pltpu.SemaphoreType.DMA((3,))],
        60,
    )(*asked)
    dn_pair = lax.ppermute(dn, "x", pair)
    arrived = lax.all_to_all(send, group, split_axis=0, concat_axis=0, tiled=True)
    rows, select = call(
        compact_kernel,
        [((r, width + LANES), bf16), ((groups, r), bf16)],
        [VMEM],
        "compact",
    )(arrived)
    rows, dn_pair, mine, own = lax.optimization_barrier((rows, dn_pair, gu, dn))
    gu_other = lax.ppermute(mine, "core", swap)
    dn_other = lax.ppermute(own, "core", swap)
    dn_both = lax.ppermute(dn_pair, "core", swap)
    got = ring(rows, n)
    steps = tuple(k for k, _ in got)
    (hid,) = call(
        functools.partial(hidden_kernel, steps),
        [((n, n * r // 2, units), bf16)],
        [SMEM, HBM, HBM] + [VMEM] * n,
        "hidden",
        [pltpu.VMEM((2,) + gu.shape, bf16), pltpu.SemaphoreType.DMA((2, CHUNKS))],
        HID,
    )(at, gu, gu_other, *[b for _, b in got])
    hid = lax.all_to_all(hid, "x", split_axis=0, concat_axis=0, tiled=True)
    (out,) = call(
        down_kernel,
        [((n, r // 2, 4 * feats), bf16)],
        [SMEM] + [VMEM] * 5,
        "down",
        room=DOWN,
    )(at, hid, dn, dn_other, dn_pair, dn_both)
    back = lax.all_to_all(out, "x", split_axis=0, concat_axis=0, tiled=True)
    (padded,) = call(spread_kernel, [((groups, 2, half), bf16)], [VMEM] * 2, "spread")(
        back, select
    )
    returned = lax.all_to_all(padded, group, split_axis=0, concat_axis=0, tiled=True)
    (mixed,) = call(mix_kernel, [((toks, width), bf16)], [VMEM] * 2, "mix")(returned, place)
    return mixed


def solution(mesh):
    fine = Mesh(mesh.devices.reshape(8, 8, 8, 2), ("y", "z", "x", "core"))
    group, local = ("y", "z"), ("x", "core")
    every = group + local
    placed = (
        P(every, None),
        P(every, None),
        P(every, None, None),
        P(group, None, local),
        P(group, None, local),
    )
    return jax.shard_map(
        shards, mesh=fine, in_specs=placed, out_specs=P(every, None), check_vma=False
    )
```

```python
import functools

import jax
import jax.numpy as jnp
from jax import lax
from jax.experimental import pallas as pl
from jax.experimental.pallas import tpu as pltpu
from jax.sharding import Mesh
from jax.sharding import PartitionSpec as P

LANES = 128
bf16, f32, i32 = jnp.bfloat16, jnp.float32, jnp.int32
VMEM = pl.BlockSpec(memory_space=pltpu.VMEM)
SMEM = pl.BlockSpec(memory_space=pltpu.SMEM)
HBM = pl.BlockSpec(memory_space=pltpu.HBM)
HID = 50
DOWN = 52
CHUNKS = 2


COSTS = {"compact": pl.CostEstimate(flops=10**10, bytes_accessed=2**24, transcendentals=0)}


def dot(a, b):
    return jnp.dot(a, b, preferred_element_type=f32)


def dot_dims(a, b, da, db):
    return lax.dot_general(a, b, (((da,), (db,)), ((), ())), preferred_element_type=f32)


def call(kernel, outs, specs, name, scratch=(), room=8):
    return pl.pallas_call(
        kernel,
        out_shape=[jax.ShapeDtypeStruct(s, d) for s, d in outs],
        in_specs=specs,
        out_specs=[VMEM] * len(outs),
        scratch_shapes=list(scratch),
        cost_estimate=COSTS.get(name),
        compiler_params=pltpu.CompilerParams(vmem_limit_bytes=room * 2**20),
        name=name,
    )


def ring(block, n):
    up = [(i, (i + 1) % n) for i in range(n)]
    down = [(i, (i - 1) % n) for i in range(n)]
    got = [(0, block)]
    fwd = back = near = block
    for k in range(1, n // 2):
        near = back
        fwd = lax.ppermute(fwd, "x", up)
        back = lax.ppermute(back, "x", down)
        got += [(k, fwd), (n - k, back)]
    twice = [(i, (i - 2) % n) for i in range(n)]
    got.append((n // 2, lax.ppermute(near, "x", twice)))
    return got


def pack_kernel(*refs):
    sources, (send_ref, place_ref), held, sems = refs[:3], refs[3:5], refs[5:8], refs[8]
    copies = [pltpu.make_async_copy(sources[i], held[i], sems.at[i]) for i in range(3)]
    for copy in copies:
        copy.start()
    picks_ref, gates_ref, tok_ref = held
    copies[0].wait()
    copies[1].wait()
    visits, toks = picks_ref.shape
    groups, _, wide = send_ref.shape
    half = wide - LANES
    node = lax.broadcasted_iota(i32, (groups, toks), 0)
    place = jnp.zeros((groups, toks), f32)
    lane = lax.broadcasted_iota(i32, (groups, LANES), 1)
    tail = jnp.zeros((groups, LANES), f32)
    for j in range(visits):
        hot = (node == picks_ref[j : j + 1, :]).astype(f32)
        place += hot
        for e in range(gates_ref.shape[1]):
            gate = jnp.sum(hot * gates_ref[j, e : e + 1, :].astype(f32), axis=1, keepdims=True)
            tail += jnp.where(lane == e, gate, 0.0)
    place = place.astype(bf16)
    place_ref[...] = place
    copies[2].wait()
    for h in range(2):
        send_ref[:, h, :half] = dot(place, tok_ref[:, h * half : (h + 1) * half]).astype(bf16)
        send_ref[:, h, half:] = tail.astype(bf16)


def by_half(hot):
    slots, k = hot.shape
    twice = jnp.broadcast_to(hot[:, None, :], (slots, 2, k)).reshape(2 * slots, k)
    parity = lax.broadcasted_iota(i32, (2 * slots, k), 0) % 2
    return jnp.concatenate([jnp.where(parity == h, twice, 0.0) for h in range(2)], axis=1).astype(
        bf16
    )


def compact_kernel(in_ref, rows_ref, select_ref):
    groups, _, wide = in_ref.shape
    half = wide - LANES
    count = rows_ref.shape[0]
    tail = in_ref[:, 0, half:]
    live = (tail.astype(f32) > 0).astype(bf16)
    low = lax.broadcasted_iota(i32, (groups, groups), 0)
    high = lax.broadcasted_iota(i32, (groups, groups), 1)
    upto = dot((high <= low).astype(bf16), live)[:, :1]
    alive = live[:, :1].astype(f32) > 0
    position = lax.broadcasted_iota(i32, (groups, count), 1).astype(f32) + 1.0
    spread = jnp.where(alive & (upto == position), 1.0, 0.0)
    select_ref[...] = spread.astype(bf16)
    both = dot_dims(by_half(spread), in_ref[...].reshape(2 * groups, wide), 0, 0).astype(bf16)
    rows_ref[:, :half] = both[:count, :half]
    rows_ref[:, half : 2 * half] = both[count:, :half]
    rows_ref[:, 2 * half :] = both[:count, half:]


def hidden_kernel(steps, at_ref, gu_ref, other_ref, *refs):
    blocks, (out_ref, buf, sems) = refs[:-3], refs[-3:]
    depth = gu_ref.shape[0] // CHUNKS
    copies = []
    for i, w in enumerate((gu_ref, other_ref)):
        for k in range(CHUNKS):
            part = pl.ds(k * depth, depth)
            copies.append(
                pltpu.make_async_copy(w.at[part, :], buf.at[i, part, :], sems.at[i, k])
            )
            copies[-1].start()
    n = len(blocks)
    x, c = at_ref[0], at_ref[1]
    r = blocks[0].shape[0]
    width = gu_ref.shape[0]
    units = gu_ref.shape[1] // 2
    hr = r // 2
    rows = jnp.concatenate([b[:, :width] for b in blocks], axis=0)
    tail = jnp.concatenate([b[:, width:] for b in blocks], axis=0).astype(f32)
    gate = jnp.where(at_ref[2] == 0, tail[:, 0:1], tail[:, 1:2])
    parts = []
    for i in range(2):
        pr = 0.0
        for k in range(CHUNKS):
            copies[i * CHUNKS + k].wait()
            lo, hi = k * depth, (k + 1) * depth
            pr += dot(rows[:, lo:hi], buf[i, lo:hi, :])
        g, p = pr[:, :units], pr[:, units:]
        parts.append((g / (1.0 + jnp.exp(-g)) * p * gate).astype(bf16))
    mine, other = parts
    first = jnp.where(c == 0, mine, other)
    second = jnp.where(c == 0, other, mine)
    h = jnp.concatenate([first, second], axis=1)
    for j, k in enumerate(steps):
        owner = lax.rem(x + (n - k), n)
        at = pl.ds(pl.multiple_of(owner * hr, hr), hr)
        for dest in range(n):
            lo = j * r + (dest % 2) * hr
            out_ref[dest, at, :] = h[lo : lo + hr]


def down_kernel(at_ref, h_ref, own_ref, other_ref, pair_ref, both_ref, out_ref):
    n, rows, units = h_ref.shape
    b, c = lax.rem(at_ref[0], 2), at_ref[1]
    h = jnp.concatenate([h_ref[k] for k in range(n)], axis=1)
    parts = [
        dot_dims(h, w[...], 1, 1).astype(bf16) for w in (own_ref, other_ref, pair_ref, both_ref)
    ]
    hr = out_ref.shape[1]
    for bb in range(2):
        for cc in range(2):

            @pl.when((b == bb) & (c == cc))
            def _():
                order = [parts[2 * (p // 2 != bb) + (p % 2 != cc)] for p in range(4)]
                whole = jnp.concatenate(order, axis=1)
                for k in range(out_ref.shape[0]):
                    out_ref[k] = whole[k * hr : (k + 1) * hr]


def spread_kernel(back_ref, select_ref, out_ref):
    n, hr, feats = back_ref.shape
    rows = [
        jnp.concatenate([back_ref[2 * a], back_ref[2 * a + 1]], axis=0) for a in range(n // 2)
    ]
    whole = jnp.concatenate(rows, axis=1)
    half = out_ref.shape[2]
    for h in range(2):
        out_ref[:, h, :] = dot(select_ref[...], whole[:, h * half : (h + 1) * half]).astype(bf16)


def mix_kernel(in_ref, place_ref, out_ref):
    slots, _, half = in_ref.shape
    toks = out_ref.shape[0]
    lhs = by_half(place_ref[...].astype(f32))
    both = dot_dims(lhs, in_ref[...].reshape(2 * slots, half), 0, 0).astype(bf16)
    out_ref[:, :half] = both[:toks]
    out_ref[:, half:] = both[toks:]


def shards(tokens, node_picks, gates, gate_up, down_weight):
    group = ("y", "z")
    groups, n = lax.axis_size(group), lax.axis_size("x")
    toks, width = tokens.shape
    visits = node_picks.shape[1]
    r = toks * visits
    half = width // 2
    x = lax.axis_index("x")
    at = jnp.stack([x, lax.axis_index("core"), x // (n // 2)]).astype(i32)
    gu, dn = gate_up[0], down_weight[0].T
    feats, units = dn.shape[0], dn.shape[1] // n
    swap = [(0, 1), (1, 0)]
    pair = [(i, i ^ 1) for i in range(n)]
    asked = (node_picks.T, gates.transpose(1, 2, 0), tokens)
    send, place = call(
        pack_kernel,
        [((groups, 2, half + LANES), bf16), ((groups, toks), bf16)],
        [HBM] * 3,
        "pack",
        [pltpu.VMEM(a.shape, a.dtype) for a in asked] + [pltpu.SemaphoreType.DMA((3,))],
        60,
    )(*asked)
    dn_pair = lax.ppermute(dn, "x", pair)
    dn_pair, mine = lax.optimization_barrier((dn_pair, gu))
    gu_other = lax.ppermute(mine, "core", swap)
    dn_other = lax.ppermute(dn, "core", swap)
    arrived = lax.all_to_all(send, group, split_axis=0, concat_axis=0, tiled=True)
    arrived, dn_other = lax.optimization_barrier((arrived, dn_other))
    rows, select = call(
        compact_kernel,
        [((r, width + LANES), bf16), ((groups, r), bf16)],
        [VMEM],
        "compact",
    )(arrived)
    got = ring(rows, n)
    steps = tuple(k for k, _ in got)
    (hid,) = call(
        functools.partial(hidden_kernel, steps),
        [((n, n * r // 2, units), bf16)],
        [SMEM, HBM, HBM] + [VMEM] * n,
        "hidden",
        [pltpu.VMEM((2,) + gu.shape, bf16), pltpu.SemaphoreType.DMA((2, CHUNKS))],
        HID,
    )(at, gu, gu_other, *[b for _, b in got])
    dn_both = lax.ppermute(dn_pair, "core", swap)
    hid = lax.all_to_all(hid, "x", split_axis=0, concat_axis=0, tiled=True)
    (out,) = call(
        down_kernel,
        [((n, r // 2, 4 * feats), bf16)],
        [SMEM] + [VMEM] * 5,
        "down",
        room=DOWN,
    )(at, hid, dn, dn_other, dn_pair, dn_both)
    back = lax.all_to_all(out, "x", split_axis=0, concat_axis=0, tiled=True)
    (padded,) = call(spread_kernel, [((groups, 2, half), bf16)], [VMEM] * 2, "spread")(
        back, select
    )
    returned = lax.all_to_all(padded, group, split_axis=0, concat_axis=0, tiled=True)
    (mixed,) = call(mix_kernel, [((toks, width), bf16)], [VMEM] * 2, "mix")(returned, place)
    return mixed


def solution(mesh):
    fine = Mesh(mesh.devices.reshape(8, 8, 8, 2), ("y", "z", "x", "core"))
    group, local = ("y", "z"), ("x", "core")
    every = group + local
    placed = (
        P(every, None),
        P(every, None),
        P(every, None, None),
        P(group, None, local),
        P(group, None, local),
    )
    return jax.shard_map(
        shards, mesh=fine, in_specs=placed, out_specs=P(every, None), check_vma=False
    )
```
